32 devices in a mesh: lon: 4 (over y, x), lat: 4 (over z), head: 2 (over core).
Axes of the slice: x: 2, y: 2, z: 4, core: 2. Of those that a mesh axis runs over, the one named last changes fastest.
Arguments:
- tokens: bfloat16 [32, 64, 1024], P('lat', 'lon'), may hold values from -60 to 60, as said below
- cotangent: bfloat16 [32, 64, 1024], P('lat', 'lon'), may hold values from -6 to 6
- w_qkv: bfloat16 [3, 1024, 1024], P(None, None, 'head'), may hold values from -0.1875 to 0.1875
- w_out: bfloat16 [1024, 1024], P('head'), may hold values from -0.1875 to 0.1875
- norm_gain: float32 [1024], replicated, may hold values from 0.1 to 1.9
- type_bias: float32 [3, 16], P(None, 'head'), may hold values from -310 to 310
- offsets: int32 [2], replicated, may hold values from 1 to 7
- window_kind: int32 [4, 8], replicated, may hold values from 0 to 2
Outputs:
- d_tokens: bfloat16 [32, 64, 1024], P('lat', 'lon')
The draws below stay inside these ranges and needn't reach their ends.
Inputs may be any that keep to these rules, and one draw needn't show every extreme that they name: `tokens`: activations of order one with scales that differ between cells and between features.
All inputs are finite; a program needn't handle non-finite values.
Results may differ from the reference program's by a relative error of at most 0.011.
Values may be sent and summed in bfloat16 or wider, within the bound.
A program may use at most 64 MiB of HBM per device.

```python
import math
import jax
import jax.numpy as jnp
from jax import lax

D = 1024
HEADS = 16
HD = 64
WIN = 8
ROWS = 32
COLS = 64


def draw_tokens(key, part):
    key = jax.random.fold_in(key, 11)
    key_base, key_cell, key_chan = jax.random.split(key, 3)
    base = jnp.clip(jax.random.normal(key_base, (ROWS, COLS, D), jnp.float32), -6.0, 6.0)
    spread = math.log(10.0)
    cell_scale = jnp.exp(jax.random.uniform(key_cell, (ROWS, COLS, 1), jnp.float32, -0.5, 0.5) * spread)
    chan_scale = jnp.exp(jax.random.uniform(key_chan, (1, 1, D), jnp.float32, -0.5, 0.5) * spread)
    return (base * cell_scale * chan_scale).astype(jnp.bfloat16)


def draw_type_bias(key, part):
    key = jax.random.fold_in(key, 23)
    key_base = jax.random.fold_in(key, 0)
    base = jnp.clip(jax.random.normal(key_base, (3, HEADS), jnp.float32) * 1.5, -9.0, 9.0)
    return base


def place_ends(entries, stream_key, smallest, high):
    place = [jax.random.randint(jax.random.fold_in(stream_key, axis), (), 0, length) for axis, length in enumerate(entries.shape)]
    longest = entries.shape.index(max(entries.shape))
    next_to = place[:longest] + [(place[longest] + 1) % entries.shape[longest]] + place[longest + 1:]
    return entries.at[tuple(place)].set(smallest).at[tuple(next_to)].set(high)


def block_scale(key, dims, cuts, low, high):
    level, own = 1.0, jax.random.fold_in(key, 6)
    for dim, parts in cuts:
        heights = jnp.exp(jax.random.uniform(jax.random.fold_in(own, dim), (parts,), jnp.float32, low / len(cuts), high / len(cuts)))
        level = level * jnp.repeat(heights, dims[dim] // parts).reshape([-1 if axis == dim else 1 for axis in range(len(dims))])
    return level


def scatter_about(rng, extent, scale, bound, cuts=(), kind=jnp.bfloat16):
    result = scale * jax.random.normal(rng, extent, jnp.float32)
    if cuts:
        result = result * block_scale(rng, extent, cuts, -0.22, 0.18)
    return jnp.clip(result, -bound, bound).astype(kind)


def setup_inputs(seed: int = 0) -> dict:
    seeds = jax.random.split(jax.random.key(seed), 9)
    tokens = draw_tokens(jax.random.fold_in(seeds[8], 71), 0)
    cotangent = scatter_about(seeds[1], (ROWS, COLS, D), 1.0, 6.0, ((0, 4), (1, 4)))
    w_qkv = scatter_about(seeds[2], (3, D, D), D ** -0.5, 0.1875, ((2, 2),))
    w_out = scatter_about(seeds[3], (D, D), D ** -0.5, 0.1875, ((0, 2),))
    norm_gain = jnp.clip(1.0 + 0.18 * jax.random.normal(seeds[4], (D,), jnp.float32), 0.1, 1.9)
    type_bias = draw_type_bias(jax.random.fold_in(seeds[8], 71), 0)
    offsets = jax.random.randint(seeds[6], (2,), 1, WIN).astype(jnp.int32)
    window_kind = place_ends(jax.random.randint(seeds[7], (ROWS // WIN, COLS // WIN), 0, 3), jax.random.fold_in(seeds[7], 1), 0, 2).astype(jnp.int32)
    return {"tokens": tokens, "cotangent": cotangent, "w_qkv": w_qkv, "w_out": w_out, "norm_gain": norm_gain, "type_bias": type_bias, "offsets": offsets, "window_kind": window_kind}


epsilon = 1e-06

def rounded(values):
    return lax.optimization_barrier(values.astype(jnp.bfloat16))

def normalize(cells, gains):
    cells_f32 = cells.astype(jnp.float32)
    inverse_rms = lax.rsqrt(lax.optimization_barrier(jnp.mean(cells_f32 * cells_f32, axis=-1, keepdims=True)) + epsilon)
    return ((cells_f32 * inverse_rms * gains).astype(jnp.bfloat16), cells_f32, inverse_rms)

def norm_back(cells_f32, inverse_rms, gains, d_normed):
    scaled = d_normed * gains
    row_inner = lax.optimization_barrier(jnp.mean(cells_f32 * scaled, axis=-1, keepdims=True))
    return inverse_rms * scaled - cells_f32 * (inverse_rms * inverse_rms * inverse_rms) * row_inner

def attend_back(q_heads, k_heads, v_heads, d_heads, key_bias, allowed, scale_val):
    q_full = q_heads.astype(jnp.float32)
    k_full = k_heads.astype(jnp.float32)
    logits = jnp.einsum('wqhe,wkhe->whqk', q_full, k_full) * scale_val
    logits = logits + jnp.transpose(key_bias, (0, 2, 1))[:, :, None, :]
    logits = jnp.where(allowed[:, None], logits, -jnp.inf)
    peak_val = lax.optimization_barrier(jnp.max(logits, axis=-1, keepdims=True))
    expo_val = jnp.exp(logits - peak_val)
    weights = expo_val / lax.optimization_barrier(jnp.sum(expo_val, axis=-1, keepdims=True))
    weights_low = rounded(weights)
    d_full = d_heads.astype(jnp.float32)
    d_values = rounded(jnp.einsum('whqk,wqhe->wkhe', weights_low.astype(jnp.float32), d_full))
    d_weights = jnp.einsum('wqhe,wkhe->whqk', d_full, v_heads.astype(jnp.float32))
    row_inner = lax.optimization_barrier(jnp.sum(weights * d_weights, axis=-1, keepdims=True))
    d_logits = rounded(scale_val * weights * (d_weights - row_inner)).astype(jnp.float32)
    d_queries = rounded(jnp.einsum('whqk,wkhe->wqhe', d_logits, k_full))
    d_keys = rounded(jnp.einsum('whqk,wqhe->wkhe', d_logits, q_full))
    return (d_queries, d_keys, d_values)

def to_windows(grid):
    row_count, col_count = (grid.shape[0], grid.shape[1])
    grid = grid.reshape((row_count // WIN, WIN, col_count // WIN, WIN) + grid.shape[2:])
    grid = jnp.moveaxis(grid, 2, 1)
    return grid.reshape((row_count // WIN, col_count // WIN, WIN * WIN) + grid.shape[4:])

def reference(tokens, cotangent, w_qkv, w_out, norm_gain, type_bias, offsets, window_kind):
    row_shift = offsets[0]
    col_shift = offsets[1]
    kind_grid = jnp.repeat(jnp.repeat(window_kind, WIN, axis=0), WIN, axis=1)
    one_hot = (kind_grid[:, :, None] == jnp.arange(3, dtype=jnp.int32)).astype(jnp.float32)
    cell_bias = jnp.einsum('rck,kh->rch', one_hot, type_bias, precision=lax.Precision.HIGHEST)

    def shift_grid(values):
        return jnp.roll(values, (-row_shift, -col_shift), axis=(0, 1))
    x_windows = to_windows(shift_grid(tokens))
    g_windows = to_windows(shift_grid(cotangent))
    b_windows = to_windows(shift_grid(cell_bias))
    w_full = w_qkv.astype(jnp.float32)

    def one_row(row_items):
        x_row, g_row, b_row, band_row = row_items
        seam_side = band_row * WIN + jnp.arange(WIN, dtype=jnp.int32) + row_shift >= ROWS
        token_side = jnp.repeat(seam_side, WIN)
        allowed = token_side[:, None] == token_side[None, :]
        allowed = jnp.broadcast_to(allowed, (x_row.shape[0], WIN * WIN, WIN * WIN))
        normed, cells_f32, inverse_rms = normalize(x_row, norm_gain)
        proj = rounded(jnp.einsum('wtd,kde->wtke', normed.astype(jnp.float32), w_full))
        head_shape = x_row.shape[:2] + (HEADS, HD)
        q_heads = proj[:, :, 0].reshape(head_shape)
        k_heads = proj[:, :, 1].reshape(head_shape)
        v_heads = proj[:, :, 2].reshape(head_shape)
        d_heads = rounded(jnp.einsum('wtd,ed->wte', g_row.astype(jnp.float32), w_out.astype(jnp.float32))).reshape(head_shape)
        d_queries, d_keys, d_values = attend_back(q_heads, k_heads, v_heads, d_heads, b_row, allowed, HD ** (-0.5))
        d_all = jnp.stack([d_queries, d_keys, d_values], axis=2).reshape(x_row.shape[:2] + (3, D))
        d_normed = jnp.einsum('wtke,kde->wtd', d_all.astype(jnp.float32), w_full)
        return (g_row.astype(jnp.float32) + norm_back(cells_f32, inverse_rms, norm_gain, d_normed)).astype(jnp.bfloat16)
    d_windows = lax.map(one_row, (x_windows, g_windows, b_windows, jnp.arange(ROWS // WIN, dtype=jnp.int32)))
    d_grid = d_windows.reshape((ROWS // WIN, COLS // WIN, WIN, WIN, D))
    d_grid = jnp.moveaxis(d_grid, 1, 2).reshape((ROWS, COLS, D))
    return jnp.roll(d_grid, (row_shift, col_shift), axis=(0, 1))
```

```python
import functools

import jax
import jax.numpy as jnp
from jax import lax
from jax.experimental import pallas as pl
from jax.experimental.pallas import tpu as pltpu
from jax.sharding import PartitionSpec as P

WIN = 8
AREA = WIN * WIN
EPSILON = 1e-06
MESH = pl.DeviceIdType.MESH
F32 = jnp.float32
BF16 = jnp.bfloat16


def dot(lhs, rhs, lhs_dim, rhs_dim):
    return lax.dot_general(
        lhs, rhs, (((lhs_dim,), (rhs_dim,)), ((), ())), preferred_element_type=F32
    )


def iota(shape, dim):
    return lax.broadcasted_iota(jnp.int32, shape, dim)


def one_hot(equal):
    return jnp.where(equal, 1.0, 0.0).astype(BF16)


def window_place(flat, row_shift, col_shift):
    row = ((flat >> 3) & 7) + row_shift
    col = ((flat >> 6) << 3) + (flat & 7) + col_shift
    return row >> 3, col >> 3, ((row & 7) << 3) + (col & 7)


def kernel(
    sizes,
    off_ref,
    kind_ref,
    bias_ref,
    gain_ref,
    tok_ref,
    cot_ref,
    wq_hbm,
    wo_hbm,
    out_ref,
    cells,
    wq,
    wo,
    proj,
    d_proj,
    part_out,
    part_in,
    ret_out,
    ret_in,
    joined,
    load_sem,
    near_send,
    near_recv,
    fwd_send,
    fwd_recv,
    part_send,
    part_recv,
    ret_send,
    ret_recv,
    join_send,
    join_recv,
):
    lons, lats, heads = sizes
    lon, lat, head = lax.axis_index("lon"), lax.axis_index("lat"), lax.axis_index("head")
    count, model = tok_ref.shape
    width = wo_hbm.shape[0]
    left, right = lax.rem(lon + lons - 1, lons), lax.rem(lon + 1, lons)
    up, down = lax.rem(lat + lats - 1, lats), lax.rem(lat + 1, lats)
    mates = [lax.rem(head + step, heads) for step in range(1, heads)]

    load_q = pltpu.make_async_copy(wq_hbm, wq, load_sem.at[0])
    load_o = pltpu.make_async_copy(wo_hbm, wo, load_sem.at[1])
    load_q.start()
    load_o.start()

    barrier = pltpu.get_barrier_semaphore()
    partners = [
        {"lon": left},
        {"lon": right},
        {"lat": up},
        {"lat": down},
        {"lon": right, "lat": down},
        {"lon": left, "lat": up},
    ] + [{"head": mate} for mate in mates]
    for partner in partners:
        pl.semaphore_signal(barrier, inc=1, device_id=partner, device_id_type=MESH)

    gain = gain_ref[...]
    tok = tok_ref[...].astype(F32)
    inverse = lax.rsqrt(jnp.mean(tok * tok, axis=-1, keepdims=True) + EPSILON)
    normed = (tok * inverse * gain).astype(BF16)
    big, small = iota((count, count), 0), iota((count, count), 1)

    def natural(flat):
        return (((flat >> 3) & 7) << 4) + ((flat >> 6) << 3) + (flat & 7)

    to_blocks = one_hot(natural(big) == small)
    from_blocks = one_hot(natural(small) == big)
    cells[0:2, 0] = dot(to_blocks, normed, 1, 0).astype(BF16).reshape(2, AREA, model)
    cells[0:2, 1] = dot(to_blocks, cot_ref[...], 1, 0).astype(BF16).reshape(2, AREA, model)

    pl.semaphore_wait(barrier, len(partners))

    share = AREA // heads
    rows = pl.ds(pl.multiple_of(head * share, share), share)

    def near(source, target, slot, device):
        return pltpu.make_async_remote_copy(
            src_ref=cells.at[source, :, rows],
            dst_ref=cells.at[target, :, rows],
            send_sem=near_send.at[slot],
            recv_sem=near_recv.at[slot],
            device_id=device,
            device_id_type=MESH,
        )

    from_below = near(0, 3, 0, {"lat": up})
    from_right = near(0, 2, 1, {"lon": left})
    from_below_next = near(1, 4, 2, {"lat": up})
    from_corner = near(3, 5, 3, {"lon": left})
    from_below.start()
    from_right.start()
    from_below_next.start()

    forwards = []

    def forward(block, slot):
        for step, mate in enumerate(mates):
            copy = pltpu.make_async_remote_copy(
                src_ref=cells.at[block, :, rows],
                dst_ref=cells.at[block, :, rows],
                send_sem=fwd_send.at[slot, step],
                recv_sem=fwd_recv.at[slot, step],
                device_id={"head": mate},
                device_id_type=MESH,
            )
            copy.start()
            forwards.append(copy)

    row_shift, col_shift = off_ref[0], off_ref[1]
    place_r = window_place(iota((count, 6 * AREA), 0), row_shift, col_shift)
    gather = one_hot(
        ((place_r[0] * 3 + place_r[1]) << 6) + place_r[2] == iota((count, 6 * AREA), 1)
    )
    place_c = window_place(iota((6 * AREA, count), 1), row_shift, col_shift)
    scatter = one_hot(
        ((place_c[0] * 3 + place_c[1]) << 6) + place_c[2] == iota((6 * AREA, count), 0)
    )

    local_heads = bias_ref.shape[1]
    head_dim = width // local_heads
    scale = head_dim ** (-0.5)
    lane_head = iota((1, width), 1) // head_dim
    kind_bias = []
    for kind in range(3):
        line = jnp.zeros((1, width), F32)
        for index in range(local_heads):
            line = jnp.where(lane_head == index, bias_ref[kind, index], line)
        kind_bias.append(line)
    group = min(width, 256)
    per_group = group // head_dim
    block_mask = one_hot(
        iota((group, group), 0) // head_dim == iota((group, group), 1) // head_dim
    )
    group_head = iota((1, group), 1) // head_dim
    query_row = (iota((AREA, group), 1) >> 3) & 7
    key_row = iota((AREA, group), 0) >> 3
    edge = lats * WIN - lat * WIN - row_shift
    allowed = (key_row >= edge) == (query_row >= edge)

    from_right.wait_recv()
    forward(2, 1)
    from_below.wait_recv()
    from_corner.start()
    forward(3, 0)
    from_below_next.wait_recv()
    forward(4, 2)
    load_q.wait()
    load_o.wait()
    from_corner.wait_recv()
    forward(5, 3)
    for copy in forwards:
        copy.wait_recv()

    picked = dot(gather, cells[:, 0].reshape(6 * AREA, model), 1, 0).astype(BF16)
    picked_cot = dot(gather, cells[:, 1].reshape(6 * AREA, model), 1, 0).astype(BF16)
    for index in range(3):
        proj[index] = dot(picked, wq[index], 1, 0).astype(BF16)
    proj[3] = dot(picked_cot, wo[...], 1, 1).astype(BF16)

    for window in range(count // AREA):
        cols = slice(window * AREA, (window + 1) * AREA)
        block_row, block_col, _ = window_place(
            iota((AREA, 1), 0) + window * AREA, row_shift, col_shift
        )
        kinds = jnp.zeros((AREA, 1), jnp.int32)
        for r in range(2):
            for c in range(3):
                kind = kind_ref[
                    lax.rem(lat + r, lats), lax.rem(lon * 2 + c, lons * 2)
                ]
                kinds = jnp.where((block_row == r) & (block_col == c), kind, kinds)
        for start in range(0, width, group):
            lanes = slice(start, start + group)
            bias = jnp.where(
                kinds == 0,
                kind_bias[0][:, lanes],
                jnp.where(kinds == 1, kind_bias[1][:, lanes], kind_bias[2][:, lanes]),
            )
            k, v = proj[1, cols, lanes], proj[2, cols, lanes]
            q_wide = jnp.concatenate([proj[0, cols, lanes]] * per_group, axis=0) * block_mask
            d_wide = jnp.concatenate([proj[3, cols, lanes]] * per_group, axis=0) * block_mask
            logits = dot(k, q_wide, 1, 1) * scale + bias
            logits = jnp.where(allowed, logits, -jnp.inf)
            expo = jnp.exp(logits - jnp.max(logits, axis=0, keepdims=True))
            weights = expo / jnp.sum(expo, axis=0, keepdims=True)
            d_weights = dot(v, d_wide, 1, 1)
            inner = jnp.sum(weights * d_weights, axis=0, keepdims=True)
            d_logits = (scale * weights * (d_weights - inner)).astype(BF16)
            d_proj[2, cols, lanes] = dot(weights.astype(BF16), d_wide, 1, 0).astype(BF16)
            d_proj[1, cols, lanes] = dot(d_logits, q_wide, 1, 0).astype(BF16)
            d_query_wide = dot(d_logits, k, 0, 0)
            d_query = jnp.zeros((AREA, group), F32)
            for index in range(per_group):
                d_query = jnp.where(
                    group_head == index,
                    d_query_wide[index * AREA : (index + 1) * AREA],
                    d_query,
                )
            d_proj[0, cols, lanes] = d_query.astype(BF16)

    slab = model // heads

    def partial_sum(owner):
        features = pl.ds(pl.multiple_of(owner * slab, slab), slab)
        total = dot(d_proj[0], wq[0, features], 1, 1)
        for index in range(1, 3):
            total = total + dot(d_proj[index], wq[index, features], 1, 1)
        return total

    parts = []
    for step, mate in enumerate(mates):
        part_out[step] = partial_sum(mate)
        copy = pltpu.make_async_remote_copy(
            src_ref=part_out.at[step],
            dst_ref=part_in.at[step],
            send_sem=part_send.at[step],
            recv_sem=part_recv.at[step],
            device_id={"head": mate},
            device_id_type=MESH,
        )
        copy.start()
        parts.append(copy)
    d_normed = partial_sum(head)
    for step, copy in enumerate(parts):
        copy.wait_recv()
        d_normed = d_normed + part_in[step]

    ret_out[...] = (
        dot(scatter, d_normed.astype(BF16), 1, 0).astype(BF16).reshape(6, AREA, slab)
    )

    def give_back(source, target, length, slot, device):
        copy = pltpu.make_async_remote_copy(
            src_ref=ret_out.at[pl.ds(source, length)],
            dst_ref=ret_in.at[pl.ds(target, length)],
            send_sem=ret_send.at[slot],
            recv_sem=ret_recv.at[slot],
            device_id=device,
            device_id_type=MESH,
        )
        copy.start()
        return copy

    returns = [
        give_back(5, 3, 1, 0, {"lon": right, "lat": down}),
        give_back(2, 0, 1, 1, {"lon": right}),
        give_back(3, 1, 2, 2, {"lat": down}),
    ]
    for copy in returns:
        copy.wait_recv()
    joined[head, 0:AREA] = ret_out[0] + ret_in[0] + ret_in[1] + ret_in[3]
    joined[head, AREA:] = ret_out[1] + ret_in[2]
    joins = []
    for step, mate in enumerate(mates):
        copy = pltpu.make_async_remote_copy(
            src_ref=joined.at[head],
            dst_ref=joined.at[head],
            send_sem=join_send.at[step],
            recv_sem=join_recv.at[step],
            device_id={"head": mate},
            device_id_type=MESH,
        )
        copy.start()
        joins.append(copy)
    for copy in joins:
        copy.wait_recv()
    whole = jnp.concatenate([joined[index] for index in range(heads)], axis=1)
    scaled = dot(from_blocks, whole, 1, 0) * gain
    tok = tok_ref[...].astype(F32)
    row_inner = jnp.mean(tok * scaled, axis=-1, keepdims=True)
    out_ref[...] = (
        cot_ref[...].astype(F32)
        + inverse * scaled
        - tok * (inverse * inverse * inverse) * row_inner
    ).astype(BF16)

    for copy in [from_below, from_right, from_below_next, from_corner]:
        copy.wait_send()
    for copy in forwards + parts + returns + joins:
        copy.wait_send()


def on_device(
    sizes, tokens, cotangent, w_qkv, w_out, norm_gain, type_bias, offsets, window_kind
):
    tile_rows, tile_cols, model = tokens.shape
    width = w_out.shape[0]
    heads = sizes[2]
    count = tile_rows * tile_cols
    mates = max(heads - 1, 1)
    slab = model // heads
    vmem = pl.BlockSpec(memory_space=pltpu.VMEM)
    smem = pl.BlockSpec(memory_space=pltpu.SMEM)
    hbm = pl.BlockSpec(memory_space=pl.ANY)
    result = pl.pallas_call(
        functools.partial(kernel, sizes),
        out_shape=jax.ShapeDtypeStruct((count, model), BF16),
        in_specs=[smem, smem, smem, vmem, vmem, vmem, hbm, hbm],
        out_specs=vmem,
        scratch_shapes=[
            pltpu.VMEM((6, 2, AREA, model), BF16),
            pltpu.VMEM(w_qkv.shape, BF16),
            pltpu.VMEM(w_out.shape, BF16),
            pltpu.VMEM((4, count, width), BF16),
            pltpu.VMEM((3, count, width), BF16),
            pltpu.VMEM((mates, count, slab), F32),
            pltpu.VMEM((mates, count, slab), F32),
            pltpu.VMEM((6, AREA, slab), BF16),
            pltpu.VMEM((4, AREA, slab), BF16),
            pltpu.VMEM((heads, count, slab), BF16),
            pltpu.SemaphoreType.DMA((2,)),
            pltpu.SemaphoreType.DMA((4,)),
            pltpu.SemaphoreType.DMA((4,)),
            pltpu.SemaphoreType.DMA((4, mates)),
            pltpu.SemaphoreType.DMA((4, mates)),
            pltpu.SemaphoreType.DMA((mates,)),
            pltpu.SemaphoreType.DMA((mates,)),
            pltpu.SemaphoreType.DMA((3,)),
            pltpu.SemaphoreType.DMA((3,)),
            pltpu.SemaphoreType.DMA((mates,)),
            pltpu.SemaphoreType.DMA((mates,)),
        ],
        compiler_params=pltpu.CompilerParams(
            collective_id=0, has_side_effects=True, vmem_limit_bytes=40 * 1024 * 1024
        ),
    )(
        offsets,
        window_kind,
        type_bias,
        norm_gain.reshape(1, model),
        tokens.reshape(count, model),
        cotangent.reshape(count, model),
        w_qkv,
        w_out,
    )
    return result.reshape(tokens.shape)


def solution(mesh):
    sizes = (mesh.shape["lon"], mesh.shape["lat"], mesh.shape["head"])
    return jax.shard_map(
        functools.partial(on_device, sizes),
        mesh=mesh,
        in_specs=(
            P("lat", "lon", None),
            P("lat", "lon", None),
            P(None, None, "head"),
            P("head", None),
            P(),
            P(None, "head"),
            P(),
            P(),
        ),
        out_specs=P("lat", "lon", None),
        check_vma=False,
    )
```

```python
import functools

import jax
import jax.numpy as jnp
from jax import lax
from jax.experimental import pallas as pl
from jax.experimental.pallas import tpu as pltpu
from jax.sharding import PartitionSpec as P

WIN = 8
AREA = WIN * WIN
EPSILON = 1e-06
MESH = pl.DeviceIdType.MESH
F32 = jnp.float32
BF16 = jnp.bfloat16


def dot(lhs, rhs, lhs_dim, rhs_dim):
    return lax.dot_general(
        lhs, rhs, (((lhs_dim,), (rhs_dim,)), ((), ())), preferred_element_type=F32
    )


def iota(shape, dim):
    return lax.broadcasted_iota(jnp.int32, shape, dim)


def one_hot(equal):
    return jnp.where(equal, 1.0, 0.0).astype(BF16)


def window_place(flat, row_shift, col_shift):
    row = ((flat >> 3) & 7) + row_shift
    col = ((flat >> 6) << 3) + (flat & 7) + col_shift
    return row >> 3, col >> 3, ((row & 7) << 3) + (col & 7)


def kernel(
    sizes,
    off_hbm,
    kind_hbm,
    bias_hbm,
    gain_hbm,
    tok_hbm,
    cot_hbm,
    wq_hbm,
    wo_hbm,
    out_ref,
    off_ref,
    kind_ref,
    bias_ref,
    gain_ref,
    tok_ref,
    cot_ref,
    cells,
    wq,
    wo,
    proj,
    d_proj,
    part_out,
    part_in,
    ret_out,
    ret_in,
    joined,
    load_sem,
    near_send,
    near_recv,
    fwd_send,
    fwd_recv,
    part_send,
    part_recv,
    ret_send,
    ret_recv,
    join_send,
    join_recv,
):
    lons, lats, heads = sizes
    lon, lat, head = lax.axis_index("lon"), lax.axis_index("lat"), lax.axis_index("head")
    count, model = tok_ref.shape
    width = wo_hbm.shape[0]
    left, right = lax.rem(lon + lons - 1, lons), lax.rem(lon + 1, lons)
    up, down = lax.rem(lat + lats - 1, lats), lax.rem(lat + 1, lats)
    mates = [lax.rem(head + step, heads) for step in range(1, heads)]

    loads = [
        pltpu.make_async_copy(source, target, load_sem.at[slot])
        for slot, (source, target) in enumerate(
            [
                (tok_hbm, tok_ref),
                (cot_hbm, cot_ref),
                (gain_hbm, gain_ref),
                (off_hbm, off_ref),
                (kind_hbm, kind_ref),
                (bias_hbm, bias_ref),
                (wq_hbm, wq),
                (wo_hbm, wo),
            ]
        )
    ]
    for load in loads:
        load.start()

    barrier = pltpu.get_barrier_semaphore()
    partners = [
        {"lon": left},
        {"lon": right},
        {"lat": up},
        {"lat": down},
    ] + [{"head": mate} for mate in mates]
    for partner in partners:
        pl.semaphore_signal(barrier, inc=1, device_id=partner, device_id_type=MESH)

    big, small = iota((count, count), 0), iota((count, count), 1)

    def natural(flat):
        return (((flat >> 3) & 7) << 4) + ((flat >> 6) << 3) + (flat & 7)

    to_blocks = one_hot(natural(big) == small)
    from_blocks = one_hot(natural(small) == big)
    loads[1].wait()
    cells[0:2, 0] = dot(to_blocks, cot_ref[...], 1, 0).astype(BF16).reshape(2, AREA, model)

    pl.semaphore_wait(barrier, len(partners))

    share = AREA // heads
    rows = pl.ds(pl.multiple_of(head * share, share), share)

    def near(source, target, array, slot, device):
        return pltpu.make_async_remote_copy(
            src_ref=cells.at[source, array, rows],
            dst_ref=cells.at[target, array, rows],
            send_sem=near_send.at[slot, array],
            recv_sem=near_recv.at[slot, array],
            device_id=device,
            device_id_type=MESH,
        )

    from_below = [near(0, 3, array, 0, {"lat": up}) for array in range(2)]
    from_right = [near(0, 2, array, 1, {"lon": left}) for array in range(2)]
    from_below_next = [near(1, 4, array, 2, {"lat": up}) for array in range(2)]
    from_corner = [near(3, 5, array, 3, {"lon": left}) for array in range(2)]
    from_below[0].start()
    from_right[0].start()

    loads[0].wait()
    loads[2].wait()
    gain = gain_ref[...]
    tok = tok_ref[...].astype(F32)
    inverse = lax.rsqrt(jnp.mean(tok * tok, axis=-1, keepdims=True) + EPSILON)
    normed = (tok * inverse * gain).astype(BF16)
    cells[0:2, 1] = dot(to_blocks, normed, 1, 0).astype(BF16).reshape(2, AREA, model)
    from_below[1].start()
    from_right[1].start()

    forwards = []

    def forward(block, array, slot):
        for step, mate in enumerate(mates):
            copy = pltpu.make_async_remote_copy(
                src_ref=cells.at[block, array, rows],
                dst_ref=cells.at[block, array, rows],
                send_sem=fwd_send.at[slot, array, step],
                recv_sem=fwd_recv.at[slot, array, step],
                device_id={"head": mate},
                device_id_type=MESH,
            )
            copy.start()
            forwards.append(copy)

    for load in loads[3:6]:
        load.wait()
    row_shift, col_shift = off_ref[0], off_ref[1]
    place_r = window_place(iota((count, 6 * AREA), 0), row_shift, col_shift)
    gather = one_hot(
        ((place_r[0] * 3 + place_r[1]) << 6) + place_r[2] == iota((count, 6 * AREA), 1)
    )
    place_c = window_place(iota((6 * AREA, count), 1), row_shift, col_shift)
    scatter = one_hot(
        ((place_c[0] * 3 + place_c[1]) << 6) + place_c[2] == iota((6 * AREA, count), 0)
    )

    local_heads = bias_ref.shape[1]
    head_dim = width // local_heads
    scale = head_dim ** (-0.5)
    lane_head = iota((1, width), 1) // head_dim
    kind_bias = []
    for kind in range(3):
        line = jnp.zeros((1, width), F32)
        for index in range(local_heads):
            line = jnp.where(lane_head == index, bias_ref[kind, index], line)
        kind_bias.append(line)
    group = min(width, 256)
    per_group = group // head_dim
    block_mask = one_hot(
        iota((group, group), 0) // head_dim == iota((group, group), 1) // head_dim
    )
    group_head = iota((1, group), 1) // head_dim
    query_row = (iota((AREA, group), 1) >> 3) & 7
    key_row = iota((AREA, group), 0) >> 3
    edge = lats * WIN - lat * WIN - row_shift
    allowed = (key_row >= edge) == (query_row >= edge)

    for array in range(2):
        from_below[array].wait_send()
        from_below_next[array].start()
    for array in range(2):
        from_below[array].wait_recv()
        from_corner[array].start()
        forward(3, array, 0)
    for array in range(2):
        from_right[array].wait_recv()
        forward(2, array, 1)
    for array in range(2):
        from_below_next[array].wait_recv()
        forward(4, array, 2)
    loads[6].wait()
    loads[7].wait()
    for array in range(2):
        from_corner[array].wait_recv()
        forward(5, array, 3)
    for copy in forwards:
        copy.wait_recv()

    picked = dot(gather, cells[:, 1].reshape(6 * AREA, model), 1, 0).astype(BF16)
    picked_cot = dot(gather, cells[:, 0].reshape(6 * AREA, model), 1, 0).astype(BF16)
    for index in range(3):
        proj[index] = dot(picked, wq[index], 1, 0).astype(BF16)
    proj[3] = dot(picked_cot, wo[...], 1, 1).astype(BF16)

    for window in range(count // AREA):
        cols = slice(window * AREA, (window + 1) * AREA)
        block_row, block_col, _ = window_place(
            iota((AREA, 1), 0) + window * AREA, row_shift, col_shift
        )
        kinds = jnp.zeros((AREA, 1), jnp.int32)
        for r in range(2):
            for c in range(3):
                kind = kind_ref[
                    lax.rem(lat + r, lats), lax.rem(lon * 2 + c, lons * 2)
                ]
                kinds = jnp.where((block_row == r) & (block_col == c), kind, kinds)
        for start in range(0, width, group):
            lanes = slice(start, start + group)
            bias = jnp.where(
                kinds == 0,
                kind_bias[0][:, lanes],
                jnp.where(kinds == 1, kind_bias[1][:, lanes], kind_bias[2][:, lanes]),
            )
            k, v = proj[1, cols, lanes], proj[2, cols, lanes]
            q_wide = jnp.concatenate([proj[0, cols, lanes]] * per_group, axis=0) * block_mask
            d_wide = jnp.concatenate([proj[3, cols, lanes]] * per_group, axis=0) * block_mask
            logits = dot(k, q_wide, 1, 1) * scale + bias
            logits = jnp.where(allowed, logits, -jnp.inf)
            expo = jnp.exp(logits - jnp.max(logits, axis=0, keepdims=True))
            weights = expo / jnp.sum(expo, axis=0, keepdims=True)
            d_weights = dot(v, d_wide, 1, 1)
            inner = jnp.sum(weights * d_weights, axis=0, keepdims=True)
            d_logits = (scale * weights * (d_weights - inner)).astype(BF16)
            d_proj[2, cols, lanes] = dot(weights.astype(BF16), d_wide, 1, 0).astype(BF16)
            d_proj[1, cols, lanes] = dot(d_logits, q_wide, 1, 0).astype(BF16)
            d_query_wide = dot(d_logits, k, 0, 0)
            d_query = jnp.zeros((AREA, group), F32)
            for index in range(per_group):
                d_query = jnp.where(
                    group_head == index,
                    d_query_wide[index * AREA : (index + 1) * AREA],
                    d_query,
                )
            d_proj[0, cols, lanes] = d_query.astype(BF16)

    slab = model // heads

    def partial_sum(owner):
        features = pl.ds(pl.multiple_of(owner * slab, slab), slab)
        total = dot(d_proj[0], wq[0, features], 1, 1)
        for index in range(1, 3):
            total = total + dot(d_proj[index], wq[index, features], 1, 1)
        return total

    parts = []
    for step, mate in enumerate(mates):
        part_out[step] = partial_sum(mate)
        copy = pltpu.make_async_remote_copy(
            src_ref=part_out.at[step],
            dst_ref=part_in.at[step],
            send_sem=part_send.at[step],
            recv_sem=part_recv.at[step],
            device_id={"head": mate},
            device_id_type=MESH,
        )
        copy.start()
        parts.append(copy)
    d_normed = partial_sum(head)
    for step, copy in enumerate(parts):
        copy.wait_recv()
        d_normed = d_normed + part_in[step]

    ret_out[...] = (
        dot(scatter, d_normed.astype(BF16), 1, 0).astype(BF16).reshape(6, AREA, slab)
    )

    def give_back(source, slot, device):
        copy = pltpu.make_async_remote_copy(
            src_ref=ret_out.at[source],
            dst_ref=ret_in.at[slot],
            send_sem=ret_send.at[slot],
            recv_sem=ret_recv.at[slot],
            device_id=device,
            device_id_type=MESH,
        )
        copy.start()
        return copy

    corner = give_back(5, 0, {"lon": right})
    next_down = give_back(4, 1, {"lat": down})
    aside = give_back(2, 2, {"lon": right})
    corner.wait_recv()
    ret_out[3] = ret_out[3] + ret_in[0]
    first_down = give_back(3, 3, {"lat": down})
    next_down.wait_recv()
    joined[head, AREA:] = ret_out[1] + ret_in[1]
    aside.wait_recv()
    first_down.wait_recv()
    joined[head, 0:AREA] = ret_out[0] + ret_in[2] + ret_in[3]
    returns = [corner, next_down, aside, first_down]
    joins = []
    for step, mate in enumerate(mates):
        copy = pltpu.make_async_remote_copy(
            src_ref=joined.at[head],
            dst_ref=joined.at[head],
            send_sem=join_send.at[step],
            recv_sem=join_recv.at[step],
            device_id={"head": mate},
            device_id_type=MESH,
        )
        copy.start()
        joins.append(copy)
    for copy in joins:
        copy.wait_recv()
    whole = jnp.concatenate([joined[index] for index in range(heads)], axis=1)
    scaled = dot(from_blocks, whole, 1, 0) * gain
    tok = tok_ref[...].astype(F32)
    row_inner = jnp.mean(tok * scaled, axis=-1, keepdims=True)
    out_ref[...] = (
        cot_ref[...].astype(F32)
        + inverse * scaled
        - tok * (inverse * inverse * inverse) * row_inner
    ).astype(BF16)

    for copy in from_right + from_below_next + from_corner:
        copy.wait_send()
    for copy in forwards + parts + returns + joins:
        copy.wait_send()


def on_device(
    sizes, tokens, cotangent, w_qkv, w_out, norm_gain, type_bias, offsets, window_kind
):
    tile_rows, tile_cols, model = tokens.shape
    width = w_out.shape[0]
    heads = sizes[2]
    count = tile_rows * tile_cols
    mates = max(heads - 1, 1)
    slab = model // heads
    vmem = pl.BlockSpec(memory_space=pltpu.VMEM)
    hbm = pl.BlockSpec(memory_space=pl.ANY)
    result = pl.pallas_call(
        functools.partial(kernel, sizes),
        out_shape=jax.ShapeDtypeStruct((count, model), BF16),
        in_specs=[hbm] * 8,
        out_specs=vmem,
        scratch_shapes=[
            pltpu.SMEM(offsets.shape, jnp.int32),
            pltpu.SMEM(window_kind.shape, jnp.int32),
            pltpu.SMEM(type_bias.shape, F32),
            pltpu.VMEM((1, model), F32),
            pltpu.VMEM((count, model), BF16),
            pltpu.VMEM((count, model), BF16),
            pltpu.VMEM((6, 2, AREA, model), BF16),
            pltpu.VMEM(w_qkv.shape, BF16),
            pltpu.VMEM(w_out.shape, BF16),
            pltpu.VMEM((4, count, width), BF16),
            pltpu.VMEM((3, count, width), BF16),
            pltpu.VMEM((mates, count, slab), F32),
            pltpu.VMEM((mates, count, slab), F32),
            pltpu.VMEM((6, AREA, slab), BF16),
            pltpu.VMEM((4, AREA, slab), BF16),
            pltpu.VMEM((heads, count, slab), BF16),
            pltpu.SemaphoreType.DMA((8,)),
            pltpu.SemaphoreType.DMA((4, 2)),
            pltpu.SemaphoreType.DMA((4, 2)),
            pltpu.SemaphoreType.DMA((4, 2, mates)),
            pltpu.SemaphoreType.DMA((4, 2, mates)),
            pltpu.SemaphoreType.DMA((mates,)),
            pltpu.SemaphoreType.DMA((mates,)),
            pltpu.SemaphoreType.DMA((4,)),
            pltpu.SemaphoreType.DMA((4,)),
            pltpu.SemaphoreType.DMA((mates,)),
            pltpu.SemaphoreType.DMA((mates,)),
        ],
        compiler_params=pltpu.CompilerParams(
            collective_id=0, has_side_effects=True, vmem_limit_bytes=63 * 1024 * 1024
        ),
    )(
        offsets,
        window_kind,
        type_bias,
        norm_gain.reshape(1, model),
        tokens.reshape(count, model),
        cotangent.reshape(count, model),
        w_qkv,
        w_out,
    )
    return result.reshape(tokens.shape)


def solution(mesh):
    sizes = (mesh.shape["lon"], mesh.shape["lat"], mesh.shape["head"])
    return jax.shard_map(
        functools.partial(on_device, sizes),
        mesh=mesh,
        in_specs=(
            P("lat", "lon", None),
            P("lat", "lon", None),
            P(None, None, "head"),
            P("head", None),
            P(),
            P(None, "head"),
            P(),
            P(),
        ),
        out_specs=P("lat", "lon", None),
        check_vma=False,
    )
```

```python
import functools

import jax
import jax.numpy as jnp
from jax import lax
from jax.experimental import pallas as pl
from jax.experimental.pallas import tpu as pltpu
from jax.sharding import PartitionSpec as P

WIN = 8
AREA = WIN * WIN
EPSILON = 1e-06
MESH = pl.DeviceIdType.MESH
F32 = jnp.float32
BF16 = jnp.bfloat16


def dot(lhs, rhs, lhs_dim, rhs_dim):
    return lax.dot_general(
        lhs, rhs, (((lhs_dim,), (rhs_dim,)), ((), ())), preferred_element_type=F32
    )


def iota(shape, dim):
    return lax.broadcasted_iota(jnp.int32, shape, dim)


def one_hot(equal):
    return jnp.where(equal, 1.0, 0.0).astype(BF16)


def window_place(flat, row_shift, col_shift):
    row = ((flat >> 3) & 7) + row_shift
    col = ((flat >> 6) << 3) + (flat & 7) + col_shift
    return row >> 3, col >> 3, ((row & 7) << 3) + (col & 7)


def kernel(
    sizes,
    off_hbm,
    kind_hbm,
    bias_hbm,
    gain_hbm,
    tok_hbm,
    cot_hbm,
    wq_hbm,
    wo_hbm,
    out_ref,
    off_ref,
    kind_ref,
    bias_ref,
    gain_ref,
    tok_ref,
    cot_ref,
    cells,
    wq,
    wo,
    proj,
    d_proj,
    part_out,
    part_in,
    extra,
    ret_out,
    ret_in,
    joined,
    load_sem,
    near_send,
    near_recv,
    fwd_send,
    fwd_recv,
    part_send,
    part_recv,
    ret_send,
    ret_recv,
    join_send,
    join_recv,
):
    lons, lats, heads = sizes
    lon, lat, head = lax.axis_index("lon"), lax.axis_index("lat"), lax.axis_index("head")
    count, model = tok_ref.shape
    width = wo_hbm.shape[0]
    left, right = lax.rem(lon + lons - 1, lons), lax.rem(lon + 1, lons)
    up, down = lax.rem(lat + lats - 1, lats), lax.rem(lat + 1, lats)
    mates = [lax.rem(head + step, heads) for step in range(1, heads)]

    loads = [
        pltpu.make_async_copy(source, target, load_sem.at[slot])
        for slot, (source, target) in enumerate(
            [
                (tok_hbm, tok_ref),
                (cot_hbm, cot_ref),
                (gain_hbm, gain_ref),
                (off_hbm, off_ref),
                (kind_hbm, kind_ref),
                (bias_hbm, bias_ref),
                (wq_hbm, wq),
                (wo_hbm, wo),
            ]
        )
    ]
    for load in loads:
        load.start()

    barrier = pltpu.get_barrier_semaphore()
    has_up, has_down = lat > 0, lat < lats - 1

    def greet(partner):
        pl.semaphore_signal(barrier, inc=1, device_id=partner, device_id_type=MESH)

    for partner in [{"lon": left}, {"lon": right}] + [{"head": mate} for mate in mates]:
        greet(partner)
    pl.when(has_up)(lambda: greet({"lat": up}))
    pl.when(has_down)(lambda: greet({"lat": down}))

    big, small = iota((count, count), 0), iota((count, count), 1)

    def natural(flat):
        return (((flat >> 3) & 7) << 4) + ((flat >> 6) << 3) + (flat & 7)

    to_blocks = one_hot(natural(big) == small)
    from_blocks = one_hot(natural(small) == big)
    loads[1].wait()
    cells[0:2, 0] = dot(to_blocks, cot_ref[...], 1, 0).astype(BF16).reshape(2, AREA, model)

    pl.semaphore_wait(
        barrier, 1 + heads + has_up.astype(jnp.int32) + has_down.astype(jnp.int32)
    )

    share = AREA // heads
    rows = pl.ds(pl.multiple_of(head * share, share), share)

    def near(source, target, array, slot, device):
        return pltpu.make_async_remote_copy(
            src_ref=cells.at[source, array, rows],
            dst_ref=cells.at[target, array, rows],
            send_sem=near_send.at[slot, array],
            recv_sem=near_recv.at[slot, array],
            device_id=device,
            device_id_type=MESH,
        )

    from_below = [near(0, 3, array, 0, {"lat": up}) for array in range(2)]
    from_right = [near(0, 2, array, 1, {"lon": left}) for array in range(2)]
    from_below_next = [near(1, 4, array, 2, {"lat": up}) for array in range(2)]
    from_corner = [near(3, 5, array, 3, {"lon": left}) for array in range(2)]
    pl.when(has_up)(from_below[0].start)
    from_right[0].start()

    loads[0].wait()
    loads[2].wait()
    gain = gain_ref[...]
    tok = tok_ref[...].astype(F32)
    inverse = lax.rsqrt(jnp.mean(tok * tok, axis=-1, keepdims=True) + EPSILON)
    normed = (tok * inverse * gain).astype(BF16)
    cells[0:2, 1] = dot(to_blocks, normed, 1, 0).astype(BF16).reshape(2, AREA, model)
    pl.when(has_up)(from_below[1].start)
    from_right[1].start()

    def forwards(block, array, slot):
        return [
            pltpu.make_async_remote_copy(
                src_ref=cells.at[block, array, rows],
                dst_ref=cells.at[block, array, rows],
                send_sem=fwd_send.at[slot, array, step],
                recv_sem=fwd_recv.at[slot, array, step],
                device_id={"head": mate},
                device_id_type=MESH,
            )
            for step, mate in enumerate(mates)
        ]

    def forward(block, array, slot):
        for copy in forwards(block, array, slot):
            copy.start()

    for load in loads[3:6]:
        load.wait()
    row_shift, col_shift = off_ref[0], off_ref[1]
    local_heads = bias_ref.shape[1]
    head_dim = width // local_heads
    scale = head_dim ** (-0.5)
    lane_head = iota((1, width), 1) // head_dim
    kind_bias = []
    for kind in range(3):
        line = jnp.zeros((1, width), F32)
        for index in range(local_heads):
            line = jnp.where(lane_head == index, bias_ref[kind, index], line)
        kind_bias.append(line)
    group = min(width, 256)
    per_group = group // head_dim
    block_mask = one_hot(
        iota((group, group), 0) // head_dim == iota((group, group), 1) // head_dim
    )
    group_head = iota((1, group), 1) // head_dim
    query_row = (iota((AREA, group), 1) >> 3) & 7
    key_row = iota((AREA, group), 0) >> 3
    slab = model // heads

    def partial_sum(owner):
        features = pl.ds(pl.multiple_of(owner * slab, slab), slab)
        total = dot(d_proj[0], wq[0, features], 1, 1)
        for index in range(1, 3):
            total = total + dot(d_proj[index], wq[index, features], 1, 1)
        return total

    def part_copies(turn):
        return [
            pltpu.make_async_remote_copy(
                src_ref=part_out.at[turn, step],
                dst_ref=part_in.at[turn, step],
                send_sem=part_send.at[turn, step],
                recv_sem=part_recv.at[turn, step],
                device_id={"head": mate},
                device_id_type=MESH,
            )
            for step, mate in enumerate(mates)
        ]

    def backward(turn, blocks, row_shift, edge):
        span = blocks * AREA
        place = window_place(iota((count, span), 0), row_shift, col_shift)
        gather = one_hot(((place[0] * 3 + place[1]) << 6) + place[2] == iota((count, span), 1))
        gather = gather * one_hot(place[0] >= 0)
        place = window_place(iota((span, count), 1), row_shift, col_shift)
        scatter = one_hot(((place[0] * 3 + place[1]) << 6) + place[2] == iota((span, count), 0))
        scatter = scatter * one_hot(place[0] >= 0)
        allowed = (key_row >= edge) == (query_row >= edge)
        picked = dot(gather, cells[0:blocks, 1].reshape(span, model), 1, 0).astype(BF16)
        picked_cot = dot(gather, cells[0:blocks, 0].reshape(span, model), 1, 0).astype(BF16)
        for index in range(3):
            proj[index] = dot(picked, wq[index], 1, 0).astype(BF16)
        proj[3] = dot(picked_cot, wo[...], 1, 1).astype(BF16)

        for window in range(count // AREA):
            cols = slice(window * AREA, (window + 1) * AREA)
            block_row, block_col, _ = window_place(
                iota((AREA, 1), 0) + window * AREA, row_shift, col_shift
            )
            kinds = jnp.zeros((AREA, 1), jnp.int32)
            for r in range(2):
                for c in range(3):
                    kind = kind_ref[
                        lax.rem(lat + r, lats), lax.rem(lon * 2 + c, lons * 2)
                    ]
                    kinds = jnp.where((block_row == r) & (block_col == c), kind, kinds)
            for start in range(0, width, group):
                lanes = slice(start, start + group)
                bias = jnp.where(
                    kinds == 0,
                    kind_bias[0][:, lanes],
                    jnp.where(kinds == 1, kind_bias[1][:, lanes], kind_bias[2][:, lanes]),
                )
                k, v = proj[1, cols, lanes], proj[2, cols, lanes]
                q_wide = jnp.concatenate([proj[0, cols, lanes]] * per_group, axis=0) * block_mask
                d_wide = jnp.concatenate([proj[3, cols, lanes]] * per_group, axis=0) * block_mask
                logits = dot(k, q_wide, 1, 1) * scale + bias
                logits = jnp.where(allowed, logits, -jnp.inf)
                expo = jnp.exp(logits - jnp.max(logits, axis=0, keepdims=True))
                weights = expo / jnp.sum(expo, axis=0, keepdims=True)
                d_weights = dot(v, d_wide, 1, 1)
                inner = jnp.sum(weights * d_weights, axis=0, keepdims=True)
                d_logits = (scale * weights * (d_weights - inner)).astype(BF16)
                d_proj[2, cols, lanes] = dot(weights.astype(BF16), d_wide, 1, 0).astype(BF16)
                d_proj[1, cols, lanes] = dot(d_logits, q_wide, 1, 0).astype(BF16)
                d_query_wide = dot(d_logits, k, 0, 0)
                d_query = jnp.zeros((AREA, group), F32)
                for index in range(per_group):
                    d_query = jnp.where(
                        group_head == index,
                        d_query_wide[index * AREA : (index + 1) * AREA],
                        d_query,
                    )
                d_proj[0, cols, lanes] = d_query.astype(BF16)

        copies = part_copies(turn)
        for step, mate in enumerate(mates):
            part_out[turn, step] = partial_sum(mate)
            copies[step].start()
        d_normed = partial_sum(head)
        for step, copy in enumerate(copies):
            copy.wait_recv()
            d_normed = d_normed + part_in[turn, step]
        spread = dot(scatter, d_normed.astype(BF16), 1, 0).astype(BF16)
        return spread.reshape(blocks, AREA, slab)

    def give_back(source, slot, device):
        return pltpu.make_async_remote_copy(
            src_ref=ret_out.at[source],
            dst_ref=ret_in.at[slot],
            send_sem=ret_send.at[slot],
            recv_sem=ret_recv.at[slot],
            device_id=device,
            device_id_type=MESH,
        )

    @pl.when(has_up)
    def _():
        for array in range(2):
            from_below[array].wait_send()
            from_below_next[array].start()

    @pl.when(has_down)
    def _():
        for array in range(2):
            from_below[array].wait_recv()
            from_corner[array].start()
            forward(3, array, 0)

    for array in range(2):
        from_right[array].wait_recv()
        forward(2, array, 1)
    loads[6].wait()
    loads[7].wait()
    for array in range(2):
        for copy in forwards(2, array, 1):
            copy.wait_recv()

    @pl.when(jnp.logical_not(has_up))
    def _():
        extra[...] = backward(1, 3, row_shift - WIN, WIN - row_shift)

    @pl.when(has_down)
    def _():
        for array in range(2):
            from_below_next[array].wait_recv()
            forward(4, array, 2)
        for array in range(2):
            from_corner[array].wait_recv()
            forward(5, array, 3)
        for block, slot in [(3, 0), (4, 2), (5, 3)]:
            for array in range(2):
                for copy in forwards(block, array, slot):
                    copy.wait_recv()

    @pl.when(jnp.logical_not(has_down))
    def _():
        cells[3:6] = jnp.zeros((3, 2, AREA, model), BF16)

    ret_out[...] = backward(0, 6, row_shift, lats * WIN - lat * WIN - row_shift)

    @pl.when(jnp.logical_not(has_up))
    def _():
        ret_out[0:3] = ret_out[0:3] + extra[...]

    corner = give_back(5, 0, {"lon": right})
    next_down = give_back(4, 1, {"lat": down})
    aside = give_back(2, 2, {"lon": right})
    first_down = give_back(3, 3, {"lat": down})

    @pl.when(has_down)
    def _():
        corner.start()
        next_down.start()

    aside.start()

    @pl.when(has_down)
    def _():
        corner.wait_recv()
        ret_out[3] = ret_out[3] + ret_in[0]
        first_down.start()

    aside.wait_recv()
    joined[head, 0:AREA] = ret_out[0] + ret_in[2]
    joined[head, AREA:] = ret_out[1]

    @pl.when(has_up)
    def _():
        next_down.wait_recv()
        joined[head, AREA:] = joined[head, AREA:] + ret_in[1]
        first_down.wait_recv()
        joined[head, 0:AREA] = joined[head, 0:AREA] + ret_in[3]

    joins = []
    for step, mate in enumerate(mates):
        copy = pltpu.make_async_remote_copy(
            src_ref=joined.at[head],
            dst_ref=joined.at[head],
            send_sem=join_send.at[step],
            recv_sem=join_recv.at[step],
            device_id={"head": mate},
            device_id_type=MESH,
        )
        copy.start()
        joins.append(copy)
    for copy in joins:
        copy.wait_recv()
    whole = jnp.concatenate([joined[index] for index in range(heads)], axis=1)
    scaled = dot(from_blocks, whole, 1, 0) * gain
    tok = tok_ref[...].astype(F32)
    row_inner = jnp.mean(tok * scaled, axis=-1, keepdims=True)
    out_ref[...] = (
        cot_ref[...].astype(F32)
        + inverse * scaled
        - tok * (inverse * inverse * inverse) * row_inner
    ).astype(BF16)

    @pl.when(has_up)
    def _():
        for copy in from_below_next:
            copy.wait_send()

    @pl.when(has_down)
    def _():
        for copy in from_corner + [corner, next_down, first_down]:
            copy.wait_send()
        for block, slot in [(3, 0), (4, 2), (5, 3)]:
            for array in range(2):
                for copy in forwards(block, array, slot):
                    copy.wait_send()

    @pl.when(jnp.logical_not(has_up))
    def _():
        for copy in part_copies(1):
            copy.wait_send()

    for array in range(2):
        for copy in forwards(2, array, 1):
            copy.wait_send()
    for copy in from_right + part_copies(0) + [aside] + joins:
        copy.wait_send()


def on_device(
    sizes, tokens, cotangent, w_qkv, w_out, norm_gain, type_bias, offsets, window_kind
):
    tile_rows, tile_cols, model = tokens.shape
    width = w_out.shape[0]
    heads = sizes[2]
    count = tile_rows * tile_cols
    mates = max(heads - 1, 1)
    slab = model // heads
    vmem = pl.BlockSpec(memory_space=pltpu.VMEM)
    hbm = pl.BlockSpec(memory_space=pl.ANY)
    result = pl.pallas_call(
        functools.partial(kernel, sizes),
        out_shape=jax.ShapeDtypeStruct((count, model), BF16),
        in_specs=[hbm] * 8,
        out_specs=vmem,
        scratch_shapes=[
            pltpu.SMEM(offsets.shape, jnp.int32),
            pltpu.SMEM(window_kind.shape, jnp.int32),
            pltpu.SMEM(type_bias.shape, F32),
            pltpu.VMEM((1, model), F32),
            pltpu.VMEM((count, model), BF16),
            pltpu.VMEM((count, model), BF16),
            pltpu.VMEM((6, 2, AREA, model), BF16),
            pltpu.VMEM(w_qkv.shape, BF16),
            pltpu.VMEM(w_out.shape, BF16),
            pltpu.VMEM((4, count, width), BF16),
            pltpu.VMEM((3, count, width), BF16),
            pltpu.VMEM((2, mates, count, slab), F32),
            pltpu.VMEM((2, mates, count, slab), F32),
            pltpu.VMEM((3, AREA, slab), BF16),
            pltpu.VMEM((6, AREA, slab), BF16),
            pltpu.VMEM((4, AREA, slab), BF16),
            pltpu.VMEM((heads, count, slab), BF16),
            pltpu.SemaphoreType.DMA((8,)),
            pltpu.SemaphoreType.DMA((4, 2)),
            pltpu.SemaphoreType.DMA((4, 2)),
            pltpu.SemaphoreType.DMA((4, 2, mates)),
            pltpu.SemaphoreType.DMA((4, 2, mates)),
            pltpu.SemaphoreType.DMA((2, mates)),
            pltpu.SemaphoreType.DMA((2, mates)),
            pltpu.SemaphoreType.DMA((4,)),
            pltpu.SemaphoreType.DMA((4,)),
            pltpu.SemaphoreType.DMA((mates,)),
            pltpu.SemaphoreType.DMA((mates,)),
        ],
        compiler_params=pltpu.CompilerParams(
            collective_id=0, has_side_effects=True, vmem_limit_bytes=63 * 1024 * 1024
        ),
    )(
        offsets,
        window_kind,
        type_bias,
        norm_gain.reshape(1, model),
        tokens.reshape(count, model),
        cotangent.reshape(count, model),
        w_qkv,
        w_out,
    )
    return result.reshape(tokens.shape)


def solution(mesh):
    sizes = (mesh.shape["lon"], mesh.shape["lat"], mesh.shape["head"])
    return jax.shard_map(
        functools.partial(on_device, sizes),
        mesh=mesh,
        in_specs=(
            P("lat", "lon", None),
            P("lat", "lon", None),
            P(None, None, "head"),
            P("head", None),
            P(),
            P(None, "head"),
            P(),
            P(),
        ),
        out_specs=P("lat", "lon", None),
        check_vma=False,
    )
```

```python
import functools

import jax
import jax.numpy as jnp
from jax import lax
from jax.experimental import pallas as pl
from jax.experimental.pallas import tpu as pltpu
from jax.sharding import PartitionSpec as P

WIN = 8
AREA = WIN * WIN
EPSILON = 1e-06
MESH = pl.DeviceIdType.MESH
F32 = jnp.float32
BF16 = jnp.bfloat16


def dot(lhs, rhs, lhs_dim, rhs_dim):
    return lax.dot_general(
        lhs, rhs, (((lhs_dim,), (rhs_dim,)), ((), ())), preferred_element_type=F32
    )


def iota(shape, dim):
    return lax.broadcasted_iota(jnp.int32, shape, dim)


def one_hot(equal):
    return jnp.where(equal, 1.0, 0.0).astype(BF16)


def window_place(flat, row_shift, col_shift):
    row = ((flat >> 3) & 7) + row_shift
    col = ((flat >> 6) << 3) + (flat & 7) + col_shift
    return row >> 3, col >> 3, ((row & 7) << 3) + (col & 7)


def kernel(
    sizes,
    off_hbm,
    kind_hbm,
    bias_hbm,
    gain_hbm,
    tok_hbm,
    cot_hbm,
    wq_hbm,
    wo_hbm,
    out_ref,
    off_ref,
    kind_ref,
    bias_ref,
    gain_ref,
    tok_ref,
    cot_ref,
    cells,
    wq,
    wo,
    proj,
    d_proj,
    part_out,
    part_in,
    part_own,
    chosen,
    extra,
    ret_out,
    ret_in,
    joined,
    load_sem,
    near_send,
    near_recv,
    fwd_send,
    fwd_recv,
    part_send,
    part_recv,
    ret_send,
    ret_recv,
    join_send,
    join_recv,
):
    lons, lats, heads = sizes
    lon, lat, head = lax.axis_index("lon"), lax.axis_index("lat"), lax.axis_index("head")
    count, model = tok_ref.shape
    width = wo_hbm.shape[0]
    left, right = lax.rem(lon + lons - 1, lons), lax.rem(lon + 1, lons)
    up, down = lax.rem(lat + lats - 1, lats), lax.rem(lat + 1, lats)
    mates = [lax.rem(head + step, heads) for step in range(1, heads)]

    loads = [
        pltpu.make_async_copy(source, target, load_sem.at[slot])
        for slot, (source, target) in enumerate(
            [
                (tok_hbm, tok_ref),
                (cot_hbm, cot_ref),
                (gain_hbm, gain_ref),
                (off_hbm, off_ref),
                (kind_hbm, kind_ref),
                (bias_hbm, bias_ref),
                (wq_hbm, wq),
                (wo_hbm, wo),
            ]
        )
    ]
    for load in loads:
        load.start()

    barrier = pltpu.get_barrier_semaphore()
    has_up, has_down = lat > 0, lat < lats - 1

    def greet(partner):
        pl.semaphore_signal(barrier, inc=1, device_id=partner, device_id_type=MESH)

    for partner in [{"lon": left}, {"lon": right}] + [{"head": mate} for mate in mates]:
        greet(partner)
    pl.when(has_up)(lambda: greet({"lat": up}))
    pl.when(has_down)(lambda: greet({"lat": down}))

    big, small = iota((count, count), 0), iota((count, count), 1)

    def natural(flat):
        return (((flat >> 3) & 7) << 4) + ((flat >> 6) << 3) + (flat & 7)

    to_blocks = one_hot(natural(big) == small)
    from_blocks = one_hot(natural(small) == big)
    loads[1].wait()
    cells[0:2, 0] = dot(to_blocks, cot_ref[...], 1, 0).astype(BF16).reshape(2, AREA, model)

    pl.semaphore_wait(
        barrier, 1 + heads + has_up.astype(jnp.int32) + has_down.astype(jnp.int32)
    )

    share = AREA // heads
    rows = pl.ds(pl.multiple_of(head * share, share), share)

    def near(source, target, array, slot, device):
        return pltpu.make_async_remote_copy(
            src_ref=cells.at[source, array, rows],
            dst_ref=cells.at[target, array, rows],
            send_sem=near_send.at[slot, array],
            recv_sem=near_recv.at[slot, array],
            device_id=device,
            device_id_type=MESH,
        )

    from_below = [near(0, 3, array, 0, {"lat": up}) for array in range(2)]
    from_right = [near(0, 2, array, 1, {"lon": left}) for array in range(2)]
    from_below_next = [near(1, 4, array, 2, {"lat": up}) for array in range(2)]
    from_corner = [near(3, 5, array, 3, {"lon": left}) for array in range(2)]
    pl.when(has_up)(from_below[0].start)
    from_right[0].start()

    loads[0].wait()
    loads[2].wait()
    gain = gain_ref[...]
    tok = tok_ref[...].astype(F32)
    inverse = lax.rsqrt(jnp.mean(tok * tok, axis=-1, keepdims=True) + EPSILON)
    normed = (tok * inverse * gain).astype(BF16)
    cells[0:2, 1] = dot(to_blocks, normed, 1, 0).astype(BF16).reshape(2, AREA, model)
    pl.when(has_up)(from_below[1].start)
    from_right[1].start()

    def forwards(block, array, slot):
        return [
            pltpu.make_async_remote_copy(
                src_ref=cells.at[block, array, rows],
                dst_ref=cells.at[block, array, rows],
                send_sem=fwd_send.at[slot, array, step],
                recv_sem=fwd_recv.at[slot, array, step],
                device_id={"head": mate},
                device_id_type=MESH,
            )
            for step, mate in enumerate(mates)
        ]

    def forward(block, array, slot):
        for copy in forwards(block, array, slot):
            copy.start()

    for load in loads[3:6]:
        load.wait()
    row_shift, col_shift = off_ref[0], off_ref[1]
    local_heads = bias_ref.shape[1]
    head_dim = width // local_heads
    scale = head_dim ** (-0.5)
    lane_head = iota((1, width), 1) // head_dim
    kind_bias = []
    for kind in range(3):
        line = jnp.zeros((1, width), F32)
        for index in range(local_heads):
            line = jnp.where(lane_head == index, bias_ref[kind, index], line)
        kind_bias.append(line)
    group = min(width, 256)
    per_group = group // head_dim
    block_mask = one_hot(
        iota((group, group), 0) // head_dim == iota((group, group), 1) // head_dim
    )
    group_head = iota((1, group), 1) // head_dim
    query_row = (iota((AREA, group), 1) >> 3) & 7
    key_row = iota((AREA, group), 0) >> 3
    slab = model // heads

    def partial_sum(owner):
        features = pl.ds(pl.multiple_of(owner * slab, slab), slab)
        total = dot(d_proj[0], wq[0, features], 1, 1)
        for index in range(1, 3):
            total = total + dot(d_proj[index], wq[index, features], 1, 1)
        return total

    def part_copies(turn):
        return [
            pltpu.make_async_remote_copy(
                src_ref=part_out.at[turn, step],
                dst_ref=part_in.at[turn, step],
                send_sem=part_send.at[turn, step],
                recv_sem=part_recv.at[turn, step],
                device_id={"head": mate},
                device_id_type=MESH,
            )
            for step, mate in enumerate(mates)
        ]

    def gather(first, last, row_shift, array):
        span = (last - first) * AREA
        block_row, block_col, inside = window_place(iota((count, span), 0), row_shift, col_shift)
        source = ((block_row * 3 + block_col) << 6) + inside
        picks = one_hot(source == iota((count, span), 1) + first * AREA)
        return dot(picks, cells[first:last, array].reshape(span, model), 1, 0).astype(BF16)

    def begin(turn, picked, picked_cot, row_shift, edge):
        allowed = (key_row >= edge) == (query_row >= edge)
        for index in range(3):
            proj[index] = dot(picked, wq[index], 1, 0).astype(BF16)
        proj[3] = dot(picked_cot, wo[...], 1, 1).astype(BF16)

        for window in range(count // AREA):
            cols = slice(window * AREA, (window + 1) * AREA)
            block_row, block_col, _ = window_place(
                iota((AREA, 1), 0) + window * AREA, row_shift, col_shift
            )
            kinds = jnp.zeros((AREA, 1), jnp.int32)
            for r in range(2):
                for c in range(3):
                    kind = kind_ref[
                        lax.rem(lat + r, lats), lax.rem(lon * 2 + c, lons * 2)
                    ]
                    kinds = jnp.where((block_row == r) & (block_col == c), kind, kinds)
            for start in range(0, width, group):
                lanes = slice(start, start + group)
                bias = jnp.where(
                    kinds == 0,
                    kind_bias[0][:, lanes],
                    jnp.where(kinds == 1, kind_bias[1][:, lanes], kind_bias[2][:, lanes]),
                )
                k, v = proj[1, cols, lanes], proj[2, cols, lanes]
                q_wide = jnp.concatenate([proj[0, cols, lanes]] * per_group, axis=0) * block_mask
                d_wide = jnp.concatenate([proj[3, cols, lanes]] * per_group, axis=0) * block_mask
                logits = dot(k, q_wide, 1, 1) * scale + bias
                logits = jnp.where(allowed, logits, -jnp.inf)
                expo = jnp.exp(logits - jnp.max(logits, axis=0, keepdims=True))
                weights = expo / jnp.sum(expo, axis=0, keepdims=True)
                d_weights = dot(v, d_wide, 1, 1)
                inner = jnp.sum(weights * d_weights, axis=0, keepdims=True)
                d_logits = (scale * weights * (d_weights - inner)).astype(BF16)
                d_proj[2, cols, lanes] = dot(weights.astype(BF16), d_wide, 1, 0).astype(BF16)
                d_proj[1, cols, lanes] = dot(d_logits, q_wide, 1, 0).astype(BF16)
                d_query_wide = dot(d_logits, k, 0, 0)
                d_query = jnp.zeros((AREA, group), F32)
                for index in range(per_group):
                    d_query = jnp.where(
                        group_head == index,
                        d_query_wide[index * AREA : (index + 1) * AREA],
                        d_query,
                    )
                d_proj[0, cols, lanes] = d_query.astype(BF16)

        copies = part_copies(turn)
        for step, mate in enumerate(mates):
            part_out[turn, step] = partial_sum(mate)
            copies[step].start()
        part_own[turn] = partial_sum(head)

    def finish(turn, blocks, row_shift):
        span = blocks * AREA
        block_row, block_col, inside = window_place(iota((span, count), 1), row_shift, col_shift)
        target = ((block_row * 3 + block_col) << 6) + inside
        scatter = one_hot(target == iota((span, count), 0))
        d_normed = part_own[turn]
        for step, copy in enumerate(part_copies(turn)):
            copy.wait_recv()
            d_normed = d_normed + part_in[turn, step]
        spread = dot(scatter, d_normed.astype(BF16), 1, 0).astype(BF16)
        return spread.reshape(blocks, AREA, slab)

    def give_back(source, slot, device):
        return pltpu.make_async_remote_copy(
            src_ref=ret_out.at[source],
            dst_ref=ret_in.at[slot],
            send_sem=ret_send.at[slot],
            recv_sem=ret_recv.at[slot],
            device_id=device,
            device_id_type=MESH,
        )

    @pl.when(has_up)
    def _():
        for array in range(2):
            from_below[array].wait_send()
            from_below_next[array].start()

    @pl.when(has_down)
    def _():
        for array in range(2):
            from_below[array].wait_recv()
            from_corner[array].start()
            forward(3, array, 0)

    for array in range(2):
        from_right[array].wait_recv()
        forward(2, array, 1)
    loads[6].wait()
    loads[7].wait()
    for array in range(2):
        for copy in forwards(2, array, 1):
            copy.wait_recv()

    @pl.when(jnp.logical_not(has_up))
    def _():
        shift = row_shift - WIN
        begin(1, gather(0, 3, shift, 1), gather(0, 3, shift, 0), shift, WIN - row_shift)

    @pl.when(jnp.logical_not(has_down))
    def _():
        cells[3:6] = jnp.zeros((3, 2, AREA, model), BF16)

    @pl.when(has_down)
    def _():
        for array in range(2):
            for copy in forwards(3, array, 0):
                copy.wait_recv()

    for array in range(2):
        chosen[array] = gather(0, 4, row_shift, array)

    @pl.when(has_down)
    def _():
        for array in range(2):
            from_below_next[array].wait_recv()
            forward(4, array, 2)
        for array in range(2):
            from_corner[array].wait_recv()
            forward(5, array, 3)
        for block, slot in [(4, 2), (5, 3)]:
            for array in range(2):
                for copy in forwards(block, array, slot):
                    copy.wait_recv()

    begin(
        0,
        chosen[1] + gather(4, 6, row_shift, 1),
        chosen[0] + gather(4, 6, row_shift, 0),
        row_shift,
        lats * WIN - lat * WIN - row_shift,
    )

    @pl.when(jnp.logical_not(has_up))
    def _():
        extra[...] = finish(1, 3, row_shift - WIN)

    ret_out[...] = finish(0, 6, row_shift)

    @pl.when(jnp.logical_not(has_up))
    def _():
        ret_out[0:3] = ret_out[0:3] + extra[...]

    corner = give_back(5, 0, {"lon": right})
    next_down = give_back(4, 1, {"lat": down})
    aside = give_back(2, 2, {"lon": right})
    first_down = give_back(3, 3, {"lat": down})

    @pl.when(has_down)
    def _():
        corner.start()
        next_down.start()

    aside.start()

    @pl.when(has_down)
    def _():
        corner.wait_recv()
        ret_out[3] = ret_out[3] + ret_in[0]
        first_down.start()

    aside.wait_recv()
    joined[head, 0:AREA] = ret_out[0] + ret_in[2]
    joined[head, AREA:] = ret_out[1]

    @pl.when(has_up)
    def _():
        next_down.wait_recv()
        joined[head, AREA:] = joined[head, AREA:] + ret_in[1]
        first_down.wait_recv()
        joined[head, 0:AREA] = joined[head, 0:AREA] + ret_in[3]

    joins = []
    for step, mate in enumerate(mates):
        copy = pltpu.make_async_remote_copy(
            src_ref=joined.at[head],
            dst_ref=joined.at[head],
            send_sem=join_send.at[step],
            recv_sem=join_recv.at[step],
            device_id={"head": mate},
            device_id_type=MESH,
        )
        copy.start()
        joins.append(copy)
    for copy in joins:
        copy.wait_recv()
    whole = jnp.concatenate([joined[index] for index in range(heads)], axis=1)
    scaled = dot(from_blocks, whole, 1, 0) * gain
    tok = tok_ref[...].astype(F32)
    row_inner = jnp.mean(tok * scaled, axis=-1, keepdims=True)
    out_ref[...] = (
        cot_ref[...].astype(F32)
        + inverse * scaled
        - tok * (inverse * inverse * inverse) * row_inner
    ).astype(BF16)

    @pl.when(has_up)
    def _():
        for copy in from_below_next:
            copy.wait_send()

    @pl.when(has_down)
    def _():
        for copy in from_corner + [corner, next_down, first_down]:
            copy.wait_send()
        for block, slot in [(3, 0), (4, 2), (5, 3)]:
            for array in range(2):
                for copy in forwards(block, array, slot):
                    copy.wait_send()

    @pl.when(jnp.logical_not(has_up))
    def _():
        for copy in part_copies(1):
            copy.wait_send()

    for array in range(2):
        for copy in forwards(2, array, 1):
            copy.wait_send()
    for copy in from_right + part_copies(0) + [aside] + joins:
        copy.wait_send()


def on_device(
    sizes, tokens, cotangent, w_qkv, w_out, norm_gain, type_bias, offsets, window_kind
):
    tile_rows, tile_cols, model = tokens.shape
    width = w_out.shape[0]
    heads = sizes[2]
    count = tile_rows * tile_cols
    mates = max(heads - 1, 1)
    slab = model // heads
    vmem = pl.BlockSpec(memory_space=pltpu.VMEM)
    hbm = pl.BlockSpec(memory_space=pl.ANY)
    result = pl.pallas_call(
        functools.partial(kernel, sizes),
        out_shape=jax.ShapeDtypeStruct((count, model), BF16),
        in_specs=[hbm] * 8,
        out_specs=vmem,
        scratch_shapes=[
            pltpu.SMEM(offsets.shape, jnp.int32),
            pltpu.SMEM(window_kind.shape, jnp.int32),
            pltpu.SMEM(type_bias.shape, F32),
            pltpu.VMEM((1, model), F32),
            pltpu.VMEM((count, model), BF16),
            pltpu.VMEM((count, model), BF16),
            pltpu.VMEM((6, 2, AREA, model), BF16),
            pltpu.VMEM(w_qkv.shape, BF16),
            pltpu.VMEM(w_out.shape, BF16),
            pltpu.VMEM((4, count, width), BF16),
            pltpu.VMEM((3, count, width), BF16),
            pltpu.VMEM((2, mates, count, slab), F32),
            pltpu.VMEM((2, mates, count, slab), F32),
            pltpu.VMEM((2, count, slab), F32),
            pltpu.VMEM((2, count, model), BF16),
            pltpu.VMEM((3, AREA, slab), BF16),
            pltpu.VMEM((6, AREA, slab), BF16),
            pltpu.VMEM((4, AREA, slab), BF16),
            pltpu.VMEM((heads, count, slab), BF16),
            pltpu.SemaphoreType.DMA((8,)),
            pltpu.SemaphoreType.DMA((4, 2)),
            pltpu.SemaphoreType.DMA((4, 2)),
            pltpu.SemaphoreType.DMA((4, 2, mates)),
            pltpu.SemaphoreType.DMA((4, 2, mates)),
            pltpu.SemaphoreType.DMA((2, mates)),
            pltpu.SemaphoreType.DMA((2, mates)),
            pltpu.SemaphoreType.DMA((4,)),
            pltpu.SemaphoreType.DMA((4,)),
            pltpu.SemaphoreType.DMA((mates,)),
            pltpu.SemaphoreType.DMA((mates,)),
        ],
        compiler_params=pltpu.CompilerParams(
            collective_id=0, has_side_effects=True, vmem_limit_bytes=63 * 1024 * 1024
        ),
    )(
        offsets,
        window_kind,
        type_bias,
        norm_gain.reshape(1, model),
        tokens.reshape(count, model),
        cotangent.reshape(count, model),
        w_qkv,
        w_out,
    )
    return result.reshape(tokens.shape)


def solution(mesh):
    sizes = (mesh.shape["lon"], mesh.shape["lat"], mesh.shape["head"])
    return jax.shard_map(
        functools.partial(on_device, sizes),
        mesh=mesh,
        in_specs=(
            P("lat", "lon", None),
            P("lat", "lon", None),
            P(None, None, "head"),
            P("head", None),
            P(),
            P(None, "head"),
            P(),
            P(),
        ),
        out_specs=P("lat", "lon", None),
        check_vma=False,
    )
```

```python
import functools

import jax
import jax.numpy as jnp
from jax import lax
from jax.experimental import pallas as pl
from jax.experimental.pallas import tpu as pltpu
from jax.sharding import PartitionSpec as P

WIN = 8
AREA = WIN * WIN
EPSILON = 1e-06
MESH = pl.DeviceIdType.MESH
F32 = jnp.float32
BF16 = jnp.bfloat16


def dot(lhs, rhs, lhs_dim, rhs_dim):
    return lax.dot_general(
        lhs, rhs, (((lhs_dim,), (rhs_dim,)), ((), ())), preferred_element_type=F32
    )


def iota(shape, dim):
    return lax.broadcasted_iota(jnp.int32, shape, dim)


def one_hot(equal):
    return jnp.where(equal, 1.0, 0.0).astype(BF16)


def window_place(flat, row_shift, col_shift):
    row = ((flat >> 3) & 7) + row_shift
    col = ((flat >> 6) << 3) + (flat & 7) + col_shift
    return row >> 3, col >> 3, ((row & 7) << 3) + (col & 7)


def kernel(
    sizes,
    off_hbm,
    kind_hbm,
    bias_hbm,
    gain_hbm,
    tok_hbm,
    cot_hbm,
    wq_hbm,
    wo_hbm,
    out_ref,
    off_ref,
    kind_ref,
    bias_ref,
    gain_ref,
    tok_ref,
    cot_ref,
    cells,
    wq,
    wo,
    proj,
    d_proj,
    part_out,
    part_in,
    part_own,
    chosen,
    extra,
    ret_out,
    ret_in,
    joined,
    load_sem,
    near_send,
    near_recv,
    fwd_send,
    fwd_recv,
    part_send,
    part_recv,
    ret_send,
    ret_recv,
    join_send,
    join_recv,
):
    lons, lats, heads = sizes
    lon, lat, head = lax.axis_index("lon"), lax.axis_index("lat"), lax.axis_index("head")
    count, model = tok_ref.shape
    width = wo_hbm.shape[0]
    left, right = lax.rem(lon + lons - 1, lons), lax.rem(lon + 1, lons)
    up, down = lax.rem(lat + lats - 1, lats), lax.rem(lat + 1, lats)
    mates = [lax.rem(head + step, heads) for step in range(1, heads)]

    loads = [
        pltpu.make_async_copy(source, target, load_sem.at[slot])
        for slot, (source, target) in enumerate(
            [
                (tok_hbm, tok_ref),
                (cot_hbm, cot_ref),
                (gain_hbm, gain_ref),
                (off_hbm, off_ref),
                (kind_hbm, kind_ref),
                (bias_hbm, bias_ref),
                (wq_hbm, wq),
                (wo_hbm, wo),
            ]
        )
    ]
    for load in loads:
        load.start()

    barrier = pltpu.get_barrier_semaphore()
    has_up, has_down = lat > 0, lat < lats - 1

    def greet(partner):
        pl.semaphore_signal(barrier, inc=1, device_id=partner, device_id_type=MESH)

    for partner in [{"lon": left}, {"lon": right}] + [{"head": mate} for mate in mates]:
        greet(partner)
    pl.when(has_up)(lambda: greet({"lat": up}))
    pl.when(has_down)(lambda: greet({"lat": down}))

    big, small = iota((count, count), 0), iota((count, count), 1)

    def natural(flat):
        return (((flat >> 3) & 7) << 4) + ((flat >> 6) << 3) + (flat & 7)

    to_blocks = one_hot(natural(big) == small)
    from_blocks = one_hot(natural(small) == big)
    loads[1].wait()
    cells[0:2, 0] = dot(to_blocks, cot_ref[...], 1, 0).astype(BF16).reshape(2, AREA, model)

    pl.semaphore_wait(
        barrier, 1 + heads + has_up.astype(jnp.int32) + has_down.astype(jnp.int32)
    )

    share = AREA // heads
    rows = pl.ds(pl.multiple_of(head * share, share), share)

    def near(source, target, array, slot, device):
        return pltpu.make_async_remote_copy(
            src_ref=cells.at[source, array, rows],
            dst_ref=cells.at[target, array, rows],
            send_sem=near_send.at[slot, array],
            recv_sem=near_recv.at[slot, array],
            device_id=device,
            device_id_type=MESH,
        )

    from_below = [near(0, 3, array, 0, {"lat": up}) for array in range(2)]
    from_right = [near(0, 2, array, 1, {"lon": left}) for array in range(2)]
    from_below_next = [near(1, 4, array, 2, {"lat": up}) for array in range(2)]
    from_corner = [near(3, 5, array, 3, {"lon": left}) for array in range(2)]
    pl.when(has_up)(from_below[0].start)
    from_right[0].start()

    loads[0].wait()
    loads[2].wait()
    gain = gain_ref[...]
    tok = tok_ref[...].astype(F32)
    inverse = lax.rsqrt(jnp.mean(tok * tok, axis=-1, keepdims=True) + EPSILON)
    normed = (tok * inverse * gain).astype(BF16)
    cells[0:2, 1] = dot(to_blocks, normed, 1, 0).astype(BF16).reshape(2, AREA, model)
    pl.when(has_up)(from_below[1].start)
    from_right[1].start()

    def forwards(block, array, slot):
        return [
            pltpu.make_async_remote_copy(
                src_ref=cells.at[block, array, rows],
                dst_ref=cells.at[block, array, rows],
                send_sem=fwd_send.at[slot, array, step],
                recv_sem=fwd_recv.at[slot, array, step],
                device_id={"head": mate},
                device_id_type=MESH,
            )
            for step, mate in enumerate(mates)
        ]

    def forward(block, array, slot):
        for copy in forwards(block, array, slot):
            copy.start()

    for load in loads[3:6]:
        load.wait()
    row_shift, col_shift = off_ref[0], off_ref[1]
    local_heads = bias_ref.shape[1]
    head_dim = width // local_heads
    scale = head_dim ** (-0.5)
    lane_head = iota((1, width), 1) // head_dim
    kind_bias = []
    for kind in range(3):
        line = jnp.zeros((1, width), F32)
        for index in range(local_heads):
            line = jnp.where(lane_head == index, bias_ref[kind, index], line)
        kind_bias.append(line)
    group = min(width, 256)
    per_group = group // head_dim
    block_mask = one_hot(
        iota((group, group), 0) // head_dim == iota((group, group), 1) // head_dim
    )
    group_head = iota((1, group), 1) // head_dim
    query_row = (iota((AREA, group), 1) >> 3) & 7
    key_row = iota((AREA, group), 0) >> 3
    slab = model // heads

    def partial_sum(owner):
        features = pl.ds(pl.multiple_of(owner * slab, slab), slab)
        total = dot(d_proj[0], wq[0, features], 1, 1)
        for index in range(1, 3):
            total = total + dot(d_proj[index], wq[index, features], 1, 1)
        return total

    def part_copies(turn):
        return [
            pltpu.make_async_remote_copy(
                src_ref=part_out.at[turn, step],
                dst_ref=part_in.at[turn, step],
                send_sem=part_send.at[turn, step],
                recv_sem=part_recv.at[turn, step],
                device_id={"head": mate},
                device_id_type=MESH,
            )
            for step, mate in enumerate(mates)
        ]

    def gather(first, last, row_shift, array):
        span = (last - first) * AREA
        block_row, block_col, inside = window_place(iota((count, span), 0), row_shift, col_shift)
        source = ((block_row * 3 + block_col) << 6) + inside
        picks = one_hot(source == iota((count, span), 1) + first * AREA)
        return dot(picks, cells[first:last, array].reshape(span, model), 1, 0).astype(BF16)

    def begin(turn, picked, picked_cot, row_shift, edge):
        allowed = (key_row >= edge) == (query_row >= edge)
        for index in range(3):
            proj[index] = dot(picked, wq[index], 1, 0).astype(BF16)
        proj[3] = dot(picked_cot, wo[...], 1, 1).astype(BF16)

        for window in range(count // AREA):
            cols = slice(window * AREA, (window + 1) * AREA)
            block_row, block_col, _ = window_place(
                iota((AREA, 1), 0) + window * AREA, row_shift, col_shift
            )
            kinds = jnp.zeros((AREA, 1), jnp.int32)
            for r in range(2):
                for c in range(3):
                    kind = kind_ref[
                        lax.rem(lat + r, lats), lax.rem(lon * 2 + c, lons * 2)
                    ]
                    kinds = jnp.where((block_row == r) & (block_col == c), kind, kinds)
            for start in range(0, width, group):
                lanes = slice(start, start + group)
                bias = jnp.where(
                    kinds == 0,
                    kind_bias[0][:, lanes],
                    jnp.where(kinds == 1, kind_bias[1][:, lanes], kind_bias[2][:, lanes]),
                )
                k, v = proj[1, cols, lanes], proj[2, cols, lanes]
                q_wide = jnp.concatenate([proj[0, cols, lanes]] * per_group, axis=0) * block_mask
                d_wide = jnp.concatenate([proj[3, cols, lanes]] * per_group, axis=0) * block_mask
                logits = dot(k, q_wide, 1, 1) * scale + bias
                logits = jnp.where(allowed, logits, -jnp.inf)
                expo = jnp.exp(logits - jnp.max(logits, axis=0, keepdims=True))
                weights = expo / jnp.sum(expo, axis=0, keepdims=True)
                d_weights = dot(v, d_wide, 1, 1)
                inner = jnp.sum(weights * d_weights, axis=0, keepdims=True)
                d_logits = (scale * weights * (d_weights - inner)).astype(BF16)
                d_proj[2, cols, lanes] = dot(weights.astype(BF16), d_wide, 1, 0).astype(BF16)
                d_proj[1, cols, lanes] = dot(d_logits, q_wide, 1, 0).astype(BF16)
                d_query_wide = dot(d_logits, k, 0, 0)
                d_query = jnp.zeros((AREA, group), F32)
                for index in range(per_group):
                    d_query = jnp.where(
                        group_head == index,
                        d_query_wide[index * AREA : (index + 1) * AREA],
                        d_query,
                    )
                d_proj[0, cols, lanes] = d_query.astype(BF16)

        copies = part_copies(turn)
        for step, mate in enumerate(mates):
            part_out[turn, step] = partial_sum(mate).astype(BF16)
            copies[step].start()
        part_own[turn] = partial_sum(head)

    def finish(turn, blocks, row_shift):
        span = blocks * AREA
        block_row, block_col, inside = window_place(iota((span, count), 1), row_shift, col_shift)
        target = ((block_row * 3 + block_col) << 6) + inside
        scatter = one_hot(target == iota((span, count), 0))
        d_normed = part_own[turn]
        for step, copy in enumerate(part_copies(turn)):
            copy.wait_recv()
            d_normed = d_normed + part_in[turn, step].astype(F32)
        spread = dot(scatter, d_normed.astype(BF16), 1, 0).astype(BF16)
        return spread.reshape(blocks, AREA, slab)

    def give_back(source, slot, device):
        return pltpu.make_async_remote_copy(
            src_ref=ret_out.at[source],
            dst_ref=ret_in.at[slot],
            send_sem=ret_send.at[slot],
            recv_sem=ret_recv.at[slot],
            device_id=device,
            device_id_type=MESH,
        )

    @pl.when(has_up)
    def _():
        for array in range(2):
            from_below[array].wait_send()
            from_below_next[array].start()

    @pl.when(has_down)
    def _():
        for array in range(2):
            from_below[array].wait_recv()
            from_corner[array].start()
            forward(3, array, 0)

    for array in range(2):
        from_right[array].wait_recv()
        forward(2, array, 1)
    loads[6].wait()
    loads[7].wait()
    for array in range(2):
        for copy in forwards(2, array, 1):
            copy.wait_recv()

    @pl.when(jnp.logical_not(has_up))
    def _():
        shift = row_shift - WIN
        begin(1, gather(0, 3, shift, 1), gather(0, 3, shift, 0), shift, WIN - row_shift)

    @pl.when(jnp.logical_not(has_down))
    def _():
        cells[3:6] = jnp.zeros((3, 2, AREA, model), BF16)

    @pl.when(has_down)
    def _():
        for array in range(2):
            for copy in forwards(3, array, 0):
                copy.wait_recv()

    for array in range(2):
        chosen[array] = gather(0, 4, row_shift, array)

    @pl.when(has_down)
    def _():
        for array in range(2):
            from_below_next[array].wait_recv()
            forward(4, array, 2)
        for array in range(2):
            from_corner[array].wait_recv()
            forward(5, array, 3)
        for block, slot in [(4, 2), (5, 3)]:
            for array in range(2):
                for copy in forwards(block, array, slot):
                    copy.wait_recv()

    begin(
        0,
        chosen[1] + gather(4, 6, row_shift, 1),
        chosen[0] + gather(4, 6, row_shift, 0),
        row_shift,
        lats * WIN - lat * WIN - row_shift,
    )

    @pl.when(jnp.logical_not(has_up))
    def _():
        extra[...] = finish(1, 3, row_shift - WIN)

    ret_out[...] = finish(0, 6, row_shift)

    @pl.when(jnp.logical_not(has_up))
    def _():
        ret_out[0:3] = ret_out[0:3] + extra[...]

    corner = give_back(5, 0, {"lon": right})
    next_down = give_back(4, 1, {"lat": down})
    aside = give_back(2, 2, {"lon": right})
    first_down = give_back(3, 3, {"lat": down})

    @pl.when(has_down)
    def _():
        corner.start()
        next_down.start()

    aside.start()

    @pl.when(has_down)
    def _():
        corner.wait_recv()
        ret_out[3] = ret_out[3] + ret_in[0]
        first_down.start()

    aside.wait_recv()
    joined[head, 0:AREA] = ret_out[0] + ret_in[2]
    joined[head, AREA:] = ret_out[1]

    @pl.when(has_up)
    def _():
        next_down.wait_recv()
        joined[head, AREA:] = joined[head, AREA:] + ret_in[1]
        first_down.wait_recv()
        joined[head, 0:AREA] = joined[head, 0:AREA] + ret_in[3]

    joins = []
    for step, mate in enumerate(mates):
        copy = pltpu.make_async_remote_copy(
            src_ref=joined.at[head],
            dst_ref=joined.at[head],
            send_sem=join_send.at[step],
            recv_sem=join_recv.at[step],
            device_id={"head": mate},
            device_id_type=MESH,
        )
        copy.start()
        joins.append(copy)
    for copy in joins:
        copy.wait_recv()
    whole = jnp.concatenate([joined[index] for index in range(heads)], axis=1)
    scaled = dot(from_blocks, whole, 1, 0) * gain
    tok = tok_ref[...].astype(F32)
    row_inner = jnp.mean(tok * scaled, axis=-1, keepdims=True)
    out_ref[...] = (
        cot_ref[...].astype(F32)
        + inverse * scaled
        - tok * (inverse * inverse * inverse) * row_inner
    ).astype(BF16)

    @pl.when(has_up)
    def _():
        for copy in from_below_next:
            copy.wait_send()

    @pl.when(has_down)
    def _():
        for copy in from_corner + [corner, next_down, first_down]:
            copy.wait_send()
        for block, slot in [(3, 0), (4, 2), (5, 3)]:
            for array in range(2):
                for copy in forwards(block, array, slot):
                    copy.wait_send()

    @pl.when(jnp.logical_not(has_up))
    def _():
        for copy in part_copies(1):
            copy.wait_send()

    for array in range(2):
        for copy in forwards(2, array, 1):
            copy.wait_send()
    for copy in from_right + part_copies(0) + [aside] + joins:
        copy.wait_send()


def on_device(
    sizes, tokens, cotangent, w_qkv, w_out, norm_gain, type_bias, offsets, window_kind
):
    tile_rows, tile_cols, model = tokens.shape
    width = w_out.shape[0]
    heads = sizes[2]
    count = tile_rows * tile_cols
    mates = max(heads - 1, 1)
    slab = model // heads
    vmem = pl.BlockSpec(memory_space=pltpu.VMEM)
    hbm = pl.BlockSpec(memory_space=pl.ANY)
    result = pl.pallas_call(
        functools.partial(kernel, sizes),
        out_shape=jax.ShapeDtypeStruct((count, model), BF16),
        in_specs=[hbm] * 8,
        out_specs=vmem,
        scratch_shapes=[
            pltpu.SMEM(offsets.shape, jnp.int32),
            pltpu.SMEM(window_kind.shape, jnp.int32),
            pltpu.SMEM(type_bias.shape, F32),
            pltpu.VMEM((1, model), F32),
            pltpu.VMEM((count, model), BF16),
            pltpu.VMEM((count, model), BF16),
            pltpu.VMEM((6, 2, AREA, model), BF16),
            pltpu.VMEM(w_qkv.shape, BF16),
            pltpu.VMEM(w_out.shape, BF16),
            pltpu.VMEM((4, count, width), BF16),
            pltpu.VMEM((3, count, width), BF16),
            pltpu.VMEM((2, mates, count, slab), BF16),
            pltpu.VMEM((2, mates, count, slab), BF16),
            pltpu.VMEM((2, count, slab), F32),
            pltpu.VMEM((2, count, model), BF16),
            pltpu.VMEM((3, AREA, slab), BF16),
            pltpu.VMEM((6, AREA, slab), BF16),
            pltpu.VMEM((4, AREA, slab), BF16),
            pltpu.VMEM((heads, count, slab), BF16),
            pltpu.SemaphoreType.DMA((8,)),
            pltpu.SemaphoreType.DMA((4, 2)),
            pltpu.SemaphoreType.DMA((4, 2)),
            pltpu.SemaphoreType.DMA((4, 2, mates)),
            pltpu.SemaphoreType.DMA((4, 2, mates)),
            pltpu.SemaphoreType.DMA((2, mates)),
            pltpu.SemaphoreType.DMA((2, mates)),
            pltpu.SemaphoreType.DMA((4,)),
            pltpu.SemaphoreType.DMA((4,)),
            pltpu.SemaphoreType.DMA((mates,)),
            pltpu.SemaphoreType.DMA((mates,)),
        ],
        compiler_params=pltpu.CompilerParams(
            collective_id=0, has_side_effects=True, vmem_limit_bytes=63 * 1024 * 1024
        ),
    )(
        offsets,
        window_kind,
        type_bias,
        norm_gain.reshape(1, model),
        tokens.reshape(count, model),
        cotangent.reshape(count, model),
        w_qkv,
        w_out,
    )
    return result.reshape(tokens.shape)


def solution(mesh):
    sizes = (mesh.shape["lon"], mesh.shape["lat"], mesh.shape["head"])
    return jax.shard_map(
        functools.partial(on_device, sizes),
        mesh=mesh,
        in_specs=(
            P("lat", "lon", None),
            P("lat", "lon", None),
            P(None, None, "head"),
            P("head", None),
            P(),
            P(None, "head"),
            P(),
            P(),
        ),
        out_specs=P("lat", "lon", None),
        check_vma=False,
    )
```

```python
import functools

import jax
import jax.numpy as jnp
from jax import lax
from jax.experimental import pallas as pl
from jax.experimental.pallas import tpu as pltpu
from jax.sharding import PartitionSpec as P

WIN = 8
AREA = WIN * WIN
EPSILON = 1e-06
MESH = pl.DeviceIdType.MESH
F32 = jnp.float32
BF16 = jnp.bfloat16


def dot(lhs, rhs, lhs_dim, rhs_dim):
    return lax.dot_general(
        lhs, rhs, (((lhs_dim,), (rhs_dim,)), ((), ())), preferred_element_type=F32
    )


def iota(shape, dim):
    return lax.broadcasted_iota(jnp.int32, shape, dim)


def one_hot(equal):
    return jnp.where(equal, 1.0, 0.0).astype(BF16)


def window_place(flat, row_shift, col_shift):
    row = ((flat >> 3) & 7) + row_shift
    col = ((flat >> 6) << 3) + (flat & 7) + col_shift
    return row >> 3, col >> 3, ((row & 7) << 3) + (col & 7)


def kernel(
    sizes,
    off_hbm,
    kind_hbm,
    bias_hbm,
    gain_hbm,
    tok_hbm,
    cot_hbm,
    wq_hbm,
    wo_hbm,
    out_ref,
    off_ref,
    kind_ref,
    bias_ref,
    gain_ref,
    tok_ref,
    cot_ref,
    cells,
    wq,
    wo,
    proj,
    d_proj,
    part_out,
    part_in,
    part_own,
    chosen,
    ret_out,
    ret_in,
    joined,
    load_sem,
    near_send,
    near_recv,
    fwd_send,
    fwd_recv,
    part_send,
    part_recv,
    ret_send,
    ret_recv,
    join_send,
    join_recv,
):
    lons, lats, heads = sizes
    lon, lat, head = lax.axis_index("lon"), lax.axis_index("lat"), lax.axis_index("head")
    count, model = tok_ref.shape
    width = wo_hbm.shape[0]
    left, right = lax.rem(lon + lons - 1, lons), lax.rem(lon + 1, lons)
    up, down = lax.rem(lat + lats - 1, lats), lax.rem(lat + 1, lats)
    mates = [lax.rem(head + step, heads) for step in range(1, heads)]

    loads = [
        pltpu.make_async_copy(source, target, load_sem.at[slot])
        for slot, (source, target) in enumerate(
            [
                (tok_hbm, tok_ref),
                (cot_hbm, cot_ref),
                (gain_hbm, gain_ref),
                (off_hbm, off_ref),
                (kind_hbm, kind_ref),
                (bias_hbm, bias_ref),
                (wq_hbm, wq),
                (wo_hbm, wo),
            ]
        )
    ]
    for load in loads:
        load.start()

    barrier = pltpu.get_barrier_semaphore()
    has_up, has_down = lat > 0, lat < lats - 1

    def greet(partner):
        pl.semaphore_signal(barrier, inc=1, device_id=partner, device_id_type=MESH)

    for partner in [{"lon": left}, {"lon": right}] + [{"head": mate} for mate in mates]:
        greet(partner)
    pl.when(has_up)(lambda: greet({"lat": up}))
    pl.when(has_down)(lambda: greet({"lat": down}))

    big, small = iota((count, count), 0), iota((count, count), 1)

    def natural(flat):
        return (((flat >> 3) & 7) << 4) + ((flat >> 6) << 3) + (flat & 7)

    to_blocks = one_hot(natural(big) == small)
    from_blocks = one_hot(natural(small) == big)
    loads[1].wait()
    cells[0:2, 0] = dot(to_blocks, cot_ref[...], 1, 0).astype(BF16).reshape(2, AREA, model)

    pl.semaphore_wait(
        barrier, 1 + heads + has_up.astype(jnp.int32) + has_down.astype(jnp.int32)
    )

    share = AREA // heads
    rows = pl.ds(pl.multiple_of(head * share, share), share)

    def near(source, target, array, slot, device):
        return pltpu.make_async_remote_copy(
            src_ref=cells.at[source, array, rows],
            dst_ref=cells.at[target, array, rows],
            send_sem=near_send.at[slot, array],
            recv_sem=near_recv.at[slot, array],
            device_id=device,
            device_id_type=MESH,
        )

    from_below = [near(0, 3, array, 0, {"lat": up}) for array in range(2)]
    from_right = [near(0, 2, array, 1, {"lon": left}) for array in range(2)]
    from_below_next = [near(1, 4, array, 2, {"lat": up}) for array in range(2)]
    from_corner = [near(3, 5, array, 3, {"lon": left}) for array in range(2)]
    pl.when(has_up)(from_below[0].start)
    from_right[0].start()

    loads[0].wait()
    loads[2].wait()
    gain = gain_ref[...]
    tok = tok_ref[...].astype(F32)
    inverse = lax.rsqrt(jnp.mean(tok * tok, axis=-1, keepdims=True) + EPSILON)
    normed = (tok * inverse * gain).astype(BF16)
    cells[0:2, 1] = dot(to_blocks, normed, 1, 0).astype(BF16).reshape(2, AREA, model)
    pl.when(has_up)(from_below[1].start)
    from_right[1].start()

    def forwards(block, array, slot):
        return [
            pltpu.make_async_remote_copy(
                src_ref=cells.at[block, array, rows],
                dst_ref=cells.at[block, array, rows],
                send_sem=fwd_send.at[slot, array, step],
                recv_sem=fwd_recv.at[slot, array, step],
                device_id={"head": mate},
                device_id_type=MESH,
            )
            for step, mate in enumerate(mates)
        ]

    def forward(block, array, slot):
        for copy in forwards(block, array, slot):
            copy.start()

    for load in loads[3:6]:
        load.wait()
    row_shift, col_shift = off_ref[0], off_ref[1]
    local_heads = bias_ref.shape[1]
    head_dim = width // local_heads
    scale = head_dim ** (-0.5)
    lane_head = iota((1, width), 1) // head_dim
    kind_bias = []
    for kind in range(3):
        line = jnp.zeros((1, width), F32)
        for index in range(local_heads):
            line = jnp.where(lane_head == index, bias_ref[kind, index], line)
        kind_bias.append(line)
    group = min(width, 256)
    per_group = group // head_dim
    block_mask = one_hot(
        iota((group, group), 0) // head_dim == iota((group, group), 1) // head_dim
    )
    group_head = iota((1, group), 1) // head_dim
    query_row = (iota((AREA, group), 1) >> 3) & 7
    key_row = iota((AREA, group), 0) >> 3
    slab = model // heads

    def partial_sum(owner):
        features = pl.ds(pl.multiple_of(owner * slab, slab), slab)
        total = dot(d_proj[0], wq[0, features], 1, 1)
        for index in range(1, 3):
            total = total + dot(d_proj[index], wq[index, features], 1, 1)
        return total

    def part_copies(turn):
        return [
            pltpu.make_async_remote_copy(
                src_ref=part_out.at[turn, step],
                dst_ref=part_in.at[turn, step],
                send_sem=part_send.at[turn, step],
                recv_sem=part_recv.at[turn, step],
                device_id={"head": mate},
                device_id_type=MESH,
            )
            for step, mate in enumerate(mates)
        ]

    def gather(first, last, row_shift, array):
        span = (last - first) * AREA
        block_row, block_col, inside = window_place(iota((count, span), 0), row_shift, col_shift)
        source = ((block_row * 3 + block_col) << 6) + inside
        picks = one_hot(source == iota((count, span), 1) + first * AREA)
        return dot(picks, cells[first:last, array].reshape(span, model), 1, 0).astype(BF16)

    def begin(turn, picked, picked_cot, row_shift, edge):
        allowed = (key_row >= edge) == (query_row >= edge)
        for index in range(3):
            proj[index] = dot(picked, wq[index], 1, 0).astype(BF16)
        proj[3] = dot(picked_cot, wo[...], 1, 1).astype(BF16)

        for window in range(count // AREA):
            cols = slice(window * AREA, (window + 1) * AREA)
            block_row, block_col, _ = window_place(
                iota((AREA, 1), 0) + window * AREA, row_shift, col_shift
            )
            kinds = jnp.zeros((AREA, 1), jnp.int32)
            for r in range(2):
                for c in range(3):
                    kind = kind_ref[
                        lax.rem(lat + r, lats), lax.rem(lon * 2 + c, lons * 2)
                    ]
                    kinds = jnp.where((block_row == r) & (block_col == c), kind, kinds)
            for start in range(0, width, group):
                lanes = slice(start, start + group)
                bias = jnp.where(
                    kinds == 0,
                    kind_bias[0][:, lanes],
                    jnp.where(kinds == 1, kind_bias[1][:, lanes], kind_bias[2][:, lanes]),
                )
                k, v = proj[1, cols, lanes], proj[2, cols, lanes]
                q_wide = jnp.concatenate([proj[0, cols, lanes]] * per_group, axis=0) * block_mask
                d_wide = jnp.concatenate([proj[3, cols, lanes]] * per_group, axis=0) * block_mask
                logits = dot(k, q_wide, 1, 1) * scale + bias
                logits = jnp.where(allowed, logits, -jnp.inf)
                expo = jnp.exp(logits - jnp.max(logits, axis=0, keepdims=True))
                weights = expo / jnp.sum(expo, axis=0, keepdims=True)
                d_weights = dot(v, d_wide, 1, 1)
                inner = jnp.sum(weights * d_weights, axis=0, keepdims=True)
                d_logits = (scale * weights * (d_weights - inner)).astype(BF16)
                d_proj[2, cols, lanes] = dot(weights.astype(BF16), d_wide, 1, 0).astype(BF16)
                d_proj[1, cols, lanes] = dot(d_logits, q_wide, 1, 0).astype(BF16)
                d_query_wide = dot(d_logits, k, 0, 0)
                d_query = jnp.zeros((AREA, group), F32)
                for index in range(per_group):
                    d_query = jnp.where(
                        group_head == index,
                        d_query_wide[index * AREA : (index + 1) * AREA],
                        d_query,
                    )
                d_proj[0, cols, lanes] = d_query.astype(BF16)

        copies = part_copies(turn)
        for step, mate in enumerate(mates):
            part_out[turn, step] = partial_sum(mate)
            copies[step].start()
        part_own[turn] = partial_sum(head)

    def finish(turn, blocks, row_shift):
        span = blocks * AREA
        block_row, block_col, inside = window_place(iota((span, count), 1), row_shift, col_shift)
        target = ((block_row * 3 + block_col) << 6) + inside
        scatter = one_hot(target == iota((span, count), 0))
        d_normed = part_own[turn]
        for step, copy in enumerate(part_copies(turn)):
            copy.wait_recv()
            d_normed = d_normed + part_in[turn, step]
        spread = dot(scatter, d_normed.astype(BF16), 1, 0).astype(BF16)
        return spread.reshape(blocks, AREA, slab)

    def give_back(source, slot, device):
        return pltpu.make_async_remote_copy(
            src_ref=ret_out.at[source],
            dst_ref=ret_in.at[slot],
            send_sem=ret_send.at[slot],
            recv_sem=ret_recv.at[slot],
            device_id=device,
            device_id_type=MESH,
        )

    @pl.when(has_up)
    def _():
        for array in range(2):
            from_below[array].wait_send()
            from_below_next[array].start()

    @pl.when(has_down)
    def _():
        for array in range(2):
            from_below[array].wait_recv()
            from_corner[array].start()
            forward(3, array, 0)

    for array in range(2):
        from_right[array].wait_recv()
        forward(2, array, 1)
    loads[6].wait()
    loads[7].wait()
    for array in range(2):
        for copy in forwards(2, array, 1):
            copy.wait_recv()

    @pl.when(jnp.logical_not(has_up))
    def _():
        shift = row_shift - WIN
        begin(1, gather(0, 3, shift, 1), gather(0, 3, shift, 0), shift, WIN - row_shift)

    @pl.when(jnp.logical_not(has_down))
    def _():
        cells[3:6] = jnp.zeros((3, 2, AREA, model), BF16)

    @pl.when(has_down)
    def _():
        for array in range(2):
            for copy in forwards(3, array, 0):
                copy.wait_recv()

    for array in range(2):
        chosen[array] = gather(0, 4, row_shift, array)

    @pl.when(has_down)
    def _():
        for array in range(2):
            from_below_next[array].wait_recv()
            forward(4, array, 2)
        for array in range(2):
            from_corner[array].wait_recv()
            forward(5, array, 3)
        for block, slot in [(4, 2), (5, 3)]:
            for array in range(2):
                for copy in forwards(block, array, slot):
                    copy.wait_recv()

    begin(
        0,
        chosen[1] + gather(4, 6, row_shift, 1),
        chosen[0] + gather(4, 6, row_shift, 0),
        row_shift,
        lats * WIN - lat * WIN - row_shift,
    )

    ret_out[...] = finish(0, 6, row_shift)

    corner = give_back(5, 0, {"lon": right})
    next_down = give_back(4, 1, {"lat": down})
    aside = give_back(2, 2, {"lon": right})
    first_down = give_back(3, 3, {"lat": down})

    @pl.when(has_down)
    def _():
        corner.start()
        next_down.start()

    @pl.when(jnp.logical_not(has_up))
    def _():
        ret_out[0:3] = ret_out[0:3] + finish(1, 3, row_shift - WIN)

    aside.start()

    @pl.when(has_down)
    def _():
        corner.wait_recv()
        ret_out[3] = ret_out[3] + ret_in[0]
        first_down.start()

    aside.wait_recv()
    joined[head, 0:AREA] = ret_out[0] + ret_in[2]
    joined[head, AREA:] = ret_out[1]

    @pl.when(has_up)
    def _():
        next_down.wait_recv()
        joined[head, AREA:] = joined[head, AREA:] + ret_in[1]
        first_down.wait_recv()
        joined[head, 0:AREA] = joined[head, 0:AREA] + ret_in[3]

    joins = []
    for step, mate in enumerate(mates):
        copy = pltpu.make_async_remote_copy(
            src_ref=joined.at[head],
            dst_ref=joined.at[head],
            send_sem=join_send.at[step],
            recv_sem=join_recv.at[step],
            device_id={"head": mate},
            device_id_type=MESH,
        )
        copy.start()
        joins.append(copy)
    for copy in joins:
        copy.wait_recv()
    whole = jnp.concatenate([joined[index] for index in range(heads)], axis=1)
    scaled = dot(from_blocks, whole, 1, 0) * gain
    tok = tok_ref[...].astype(F32)
    row_inner = jnp.mean(tok * scaled, axis=-1, keepdims=True)
    out_ref[...] = (
        cot_ref[...].astype(F32)
        + inverse * scaled
        - tok * (inverse * inverse * inverse) * row_inner
    ).astype(BF16)

    @pl.when(has_up)
    def _():
        for copy in from_below_next:
            copy.wait_send()

    @pl.when(has_down)
    def _():
        for copy in from_corner + [corner, next_down, first_down]:
            copy.wait_send()
        for block, slot in [(3, 0), (4, 2), (5, 3)]:
            for array in range(2):
                for copy in forwards(block, array, slot):
                    copy.wait_send()

    @pl.when(jnp.logical_not(has_up))
    def _():
        for copy in part_copies(1):
            copy.wait_send()

    for array in range(2):
        for copy in forwards(2, array, 1):
            copy.wait_send()
    for copy in from_right + part_copies(0) + [aside] + joins:
        copy.wait_send()


def on_device(
    sizes, tokens, cotangent, w_qkv, w_out, norm_gain, type_bias, offsets, window_kind
):
    tile_rows, tile_cols, model = tokens.shape
    width = w_out.shape[0]
    heads = sizes[2]
    count = tile_rows * tile_cols
    mates = max(heads - 1, 1)
    slab = model // heads
    vmem = pl.BlockSpec(memory_space=pltpu.VMEM)
    hbm = pl.BlockSpec(memory_space=pl.ANY)
    result = pl.pallas_call(
        functools.partial(kernel, sizes),
        out_shape=jax.ShapeDtypeStruct((count, model), BF16),
        in_specs=[hbm] * 8,
        out_specs=vmem,
        scratch_shapes=[
            pltpu.SMEM(offsets.shape, jnp.int32),
            pltpu.SMEM(window_kind.shape, jnp.int32),
            pltpu.SMEM(type_bias.shape, F32),
            pltpu.VMEM((1, model), F32),
            pltpu.VMEM((count, model), BF16),
            pltpu.VMEM((count, model), BF16),
            pltpu.VMEM((6, 2, AREA, model), BF16),
            pltpu.VMEM(w_qkv.shape, BF16),
            pltpu.VMEM(w_out.shape, BF16),
            pltpu.VMEM((4, count, width), BF16),
            pltpu.VMEM((3, count, width), BF16),
            pltpu.VMEM((2, mates, count, slab), F32),
            pltpu.VMEM((2, mates, count, slab), F32),
            pltpu.VMEM((2, count, slab), F32),
            pltpu.VMEM((2, count, model), BF16),
            pltpu.VMEM((6, AREA, slab), BF16),
            pltpu.VMEM((4, AREA, slab), BF16),
            pltpu.VMEM((heads, count, slab), BF16),
            pltpu.SemaphoreType.DMA((8,)),
            pltpu.SemaphoreType.DMA((4, 2)),
            pltpu.SemaphoreType.DMA((4, 2)),
            pltpu.SemaphoreType.DMA((4, 2, mates)),
            pltpu.SemaphoreType.DMA((4, 2, mates)),
            pltpu.SemaphoreType.DMA((2, mates)),
            pltpu.SemaphoreType.DMA((2, mates)),
            pltpu.SemaphoreType.DMA((4,)),
            pltpu.SemaphoreType.DMA((4,)),
            pltpu.SemaphoreType.DMA((mates,)),
            pltpu.SemaphoreType.DMA((mates,)),
        ],
        compiler_params=pltpu.CompilerParams(
            collective_id=0, has_side_effects=True, vmem_limit_bytes=63 * 1024 * 1024
        ),
    )(
        offsets,
        window_kind,
        type_bias,
        norm_gain.reshape(1, model),
        tokens.reshape(count, model),
        cotangent.reshape(count, model),
        w_qkv,
        w_out,
    )
    return result.reshape(tokens.shape)


def solution(mesh):
    sizes = (mesh.shape["lon"], mesh.shape["lat"], mesh.shape["head"])
    return jax.shard_map(
        functools.partial(on_device, sizes),
        mesh=mesh,
        in_specs=(
            P("lat", "lon", None),
            P("lat", "lon", None),
            P(None, None, "head"),
            P("head", None),
            P(),
            P(None, "head"),
            P(),
            P(),
        ),
        out_specs=P("lat", "lon", None),
        check_vma=False,
    )
```
